128 devices in a mesh: ctx: 4 (over x), batch: 32 (over z, y, core).
Axes of the slice: x: 4, y: 4, z: 4, core: 2. Of those that a mesh axis runs over, the one named last changes fastest.
Arguments:
- queries: bfloat16 [32, 2, 32, 512], P('batch', None, 'ctx'), may hold values from -32 to 32
- latent_cache: bfloat16 [32, 2, 4096, 512], P('batch', None, 'ctx'), may hold values from -4 to 4
- token_latent: bfloat16 [32, 2, 512], P('batch'), may hold values from -4 to 4
- lengths: int32 [32, 2], P('batch'), may hold values from 512 to 4096, as said below
- value_up_weight: bfloat16 [32, 512, 128], P('ctx'), may hold values from -0.25 to 0.25
- out_proj: bfloat16 [4096, 2304], P('ctx'), may hold values from -0.09375 to 0.09375
- residual: bfloat16 [32, 2, 2304], P('batch'), may hold values from -6 to 6
- norm_gain: bfloat16 [2304], replicated, may hold values from 0.5 to 1.5
- router: bfloat16 [2304, 128], replicated, may hold values from -0.125 to 0.125
- expert_ids: int32 [32, 2, 8], replicated, may hold values from 0 to 127, all different within a row; in each aligned block of 64 rows (0 to 63, 64 to 127, ..., all dimensions but the last counted through in order) at most 8 rows name the same one
- expert_gate_up: bfloat16 [128, 2304, 2048], P(('ctx', 'batch')), may hold values from -0.125 to 0.125
- expert_down: bfloat16 [128, 1024, 2304], P(('ctx', 'batch')), may hold values from -0.1875 to 0.1875
- shared_gate_up: bfloat16 [2, 2304, 1024], P(None, None, 'ctx'), may hold values from -0.125 to 0.125
- shared_down: bfloat16 [1024, 2304], P('ctx'), may hold values from -0.1875 to 0.1875
Outputs:
- layer_out: bfloat16 [32, 2, 2304], P('batch')
The draws below stay inside these ranges and needn't reach their ends.
Inputs may be any that keep to these rules, and one draw needn't show every extreme that they name: `lengths`: each block of 2 rows along the second dimension has a row with all 4096 positions valid. `expert_ids`: each row names 8 different experts; over all 64 rows no expert is named by more than 8 rows, a bound that some block reaches.
All inputs are finite; a program needn't handle non-finite values.
Results may differ from the reference program's by a relative error of at most 0.012.
Values may be sent and summed in bfloat16 or wider, within the bound.
No kernel may reach another device: no remote copies, remote signals or barrier semaphores. Data moves between devices by JAX's collectives and lax.ppermute only.
A program may use at most 128 MiB of HBM per device.

```python
import math
import jax
import jax.numpy as jnp
import numpy as np
from jax import lax

D = 2304
ATTENTION_HEADS = 32
LATENT_WIDTH = 512
VALUE_WIDTH = 128
QK = 192
MOE_FF = 1024
TOPK = 8
EXPERTS = 128
ROWS_PER_BATCH = 2
CONTEXT_PER_PART = 1024
ROWS = 64
CACHE_POSITIONS = 4096
MIN_LEN = 512
CAP = 8
N_CTX = 4
N_BATCH = 32


def shared_base(key):
    inner = jax.random.fold_in(key, 101)
    leading_key = jax.random.fold_in(inner, 0)
    base_offset = jnp.clip(jax.random.normal(leading_key, (N_BATCH, ROWS_PER_BATCH, CACHE_POSITIONS, LATENT_WIDTH), jnp.float32), -4.0, 4.0)
    return base_offset


def token_base(key):
    inner = jax.random.fold_in(key, 103)
    return jnp.clip(jax.random.normal(inner, (N_BATCH, ROWS_PER_BATCH, LATENT_WIDTH), jnp.float32), -4.0, 4.0)


def block_means(low_scale, high_scale, raw):
    block_place = jnp.arange(N_CTX, dtype=jnp.float32) / max(N_CTX - 1, 1)
    scales = low_scale + (high_scale - low_scale) * block_place
    means = raw * scales[None, None, :, None]
    return jnp.repeat(means, CONTEXT_PER_PART, axis=2)


def draw_latent_cache(key, part):
    base_offset = shared_base(key)
    key = jax.random.fold_in(key, 3)
    offset_key = jax.random.fold_in(key, 17)
    mean_layout = (N_BATCH, ROWS_PER_BATCH, N_CTX, LATENT_WIDTH)
    cache = base_offset
    raw = jnp.clip(jax.random.normal(offset_key, mean_layout, jnp.float32), -3.0, 3.0)
    cache = cache + block_means(0.4, 1.2, raw)
    return jnp.clip(cache, -4.0, 4.0).astype(jnp.bfloat16)


def draw_token_latent(key, part):
    return token_base(key).astype(jnp.bfloat16)


def draw_queries(key, part):
    key = jax.random.fold_in(key, 5)
    leading_key = jax.random.fold_in(key, 0)
    query_layout = (N_BATCH, ROWS_PER_BATCH, ATTENTION_HEADS, LATENT_WIDTH)
    values = 0.5 * jnp.clip(jax.random.normal(leading_key, query_layout, jnp.float32), -6.0, 6.0)
    return jnp.clip(values, -32.0, 32.0).astype(jnp.bfloat16)


def draw_lengths(key, part):
    key = jax.random.fold_in(key, 9)
    leading_key, second_key = jax.random.split(key)
    drawn = jax.random.randint(leading_key, (N_BATCH, ROWS_PER_BATCH), MIN_LEN, CACHE_POSITIONS + 1)
    longest = jax.random.randint(second_key, (N_BATCH, 1), 0, ROWS_PER_BATCH)
    return jnp.where(jnp.arange(ROWS_PER_BATCH)[None, :] == longest, CACHE_POSITIONS, drawn).astype(jnp.int32)


def block_scale(own_key, extent, cuts, low, top_value):
    factor_of, own = 1.0, jax.random.fold_in(own_key, 6)
    for axis_at, shards_of in cuts:
        steps = jnp.exp(jax.random.uniform(jax.random.fold_in(own, axis_at), (shards_of,), jnp.float32, low / len(cuts), top_value / len(cuts)))
        factor_of = factor_of * jnp.repeat(steps, extent[axis_at] // shards_of).reshape([-1 if axis == axis_at else 1 for axis in range(len(extent))])
    return factor_of


def deal_out(key, own, number, rows, count, top, reach, lean):
    ranking = jax.random.permutation(key, count)
    crowded, ordinary = shares(count, rows * top, reach, lean, True), shares(count, rows * top, reach, lean, False)
    places = jnp.arange(count)

    def named(sizes, turn):
        used = int((sizes > 0).sum())
        fixed = max(1, used // 4)
        shifted = fixed + (places - fixed + turn * (used - fixed)) % max(1, count - fixed)
        return jnp.zeros((count,), jnp.int32).at[ranking[jnp.where(places < fixed, places, shifted)]].set(jnp.asarray(sizes, jnp.int32))

    sizes = jnp.where(number % 4 == 0, named(crowded, number // 4), named(ordinary, number - number // 4 - 1))
    mixed = jax.random.permutation(jax.random.fold_in(own, 3), count)
    giver, sink = mixed[0:count // 2 * 2:2], mixed[1:count // 2 * 2:2]
    margin = jnp.minimum(sizes[giver] - 1, reach - sizes[sink]) // 2
    margin = jnp.where((giver == ranking[0]) | (sink == ranking[0]) | (sizes[sink] == 0), 0, jnp.maximum(margin, 0))
    shifted = jax.random.randint(jax.random.fold_in(own, 4), (count // 2,), 0, 1 << 20) % (margin + 1)
    sizes = sizes.at[giver].add(-shifted).at[sink].add(shifted)
    labels = jnp.searchsorted(jnp.cumsum(sizes), jnp.arange(rows * top), side="right").astype(jnp.int32)
    listing = labels.reshape(top, rows).T
    listing = listing[jax.random.permutation(jax.random.fold_in(own, 1), rows)]
    turn = jax.random.randint(jax.random.fold_in(own, 2), (rows, 1), 0, top)
    return jnp.take_along_axis(listing, (jnp.arange(top)[None, :] + turn) % top, axis=1)


def shares(number_of, total, bound, skew, full):
    portions = [(1 << 20) // math.isqrt(rank ** skew) + 1 for rank in range(1, number_of + 1)]
    largest = bound if full else min(bound, max(-(-total // number_of), total * portions[0] // sum(portions)))
    least = 1 if total - largest >= number_of - 1 else 0
    holding, surplus = [largest] + [least] * (number_of - 1), total - largest - least * (number_of - 1)
    while surplus > 0:
        free = [i for i in range(1, number_of) if holding[i] < largest] or [i for i in range(1, number_of) if holding[i] < bound]
        whole, left = sum([portions[i] for i in free]), surplus
        for i in free:
            extra = min(bound - holding[i], max(1, left * portions[i] // whole), surplus)
            holding[i] = holding[i] + extra
            surplus = surplus - extra
    return np.array(holding)


def gaussian(own_key, dims, width, reach, cuts=(), kind=jnp.bfloat16):
    entries = width * jax.random.normal(own_key, dims, jnp.float32)
    if cuts:
        entries = entries * block_scale(own_key, dims, cuts, -0.22, 0.18)
    return jnp.clip(entries, -reach, reach).astype(kind)


def setup_inputs(seed: int = 0) -> dict:
    splits = jax.random.split(jax.random.key(seed), 15)
    queries = draw_queries(jax.random.fold_in(splits[14], 71), 0)
    latent_cache = draw_latent_cache(jax.random.fold_in(splits[14], 71), 0)
    token_latent = draw_token_latent(jax.random.fold_in(splits[14], 71), 0)
    lengths = draw_lengths(jax.random.fold_in(splits[14], 71), 0)
    value_up_weight = gaussian(splits[4], (ATTENTION_HEADS, LATENT_WIDTH, VALUE_WIDTH), LATENT_WIDTH ** -0.5, 0.25, ((0, 4),))
    out_proj = gaussian(splits[5], (ATTENTION_HEADS * VALUE_WIDTH, D), (ATTENTION_HEADS * VALUE_WIDTH) ** -0.5, 0.09375, ((0, 4),))
    residual = gaussian(splits[6], (N_BATCH, ROWS_PER_BATCH, D), 1.0, 6.0, ((0, 32),))
    norm_gain = jnp.clip(1.0 + 0.1 * jax.random.normal(splits[7], (D,), jnp.float32), 0.5, 1.5).astype(jnp.bfloat16)
    router = gaussian(splits[8], (D, EXPERTS), D ** -0.5, 0.125)
    expert_ids_keys = jax.random.split(jax.random.fold_in(splits[9], 1), N_BATCH * ROWS_PER_BATCH // ROWS)
    expert_ids_turns = jax.random.permutation(jax.random.fold_in(splits[9], 3), N_BATCH * ROWS_PER_BATCH // ROWS)
    expert_ids = jax.vmap(lambda own, number: deal_out(jax.random.fold_in(splits[9], 2), own, number, ROWS, EXPERTS, TOPK, CAP, 2))(expert_ids_keys, expert_ids_turns).reshape((N_BATCH, ROWS_PER_BATCH, TOPK))
    expert_gate_up = gaussian(splits[10], (EXPERTS, D, 2 * MOE_FF), D ** -0.5, 0.125, ((0, 128),))
    expert_down = gaussian(splits[11], (EXPERTS, MOE_FF, D), MOE_FF ** -0.5, 0.1875, ((0, 128),))
    shared_gate_up = gaussian(splits[12], (2, D, MOE_FF), D ** -0.5, 0.125, ((2, 4),))
    shared_down = gaussian(splits[13], (MOE_FF, D), MOE_FF ** -0.5, 0.1875, ((0, 4),))
    return {"queries": queries, "latent_cache": latent_cache, "token_latent": token_latent, "lengths": lengths, "value_up_weight": value_up_weight, "out_proj": out_proj, "residual": residual, "norm_gain": norm_gain, "router": router, "expert_ids": expert_ids, "expert_gate_up": expert_gate_up, "expert_down": expert_down, "shared_gate_up": shared_gate_up, "shared_down": shared_down}


NEG_FILL = -1e+30
ROUTE_SCALE = 2.446
EPSILON = 1e-06

def attend_group(group_args, value_up_weight, out_proj, norm_gain, router, shared_gate_up, shared_down):
    query_rows, latents, row_lengths, fresh, residual_rows, picks = group_args
    row_number = query_rows.shape[0]
    score_scale = QK ** (-0.5)
    query_f = query_rows.astype(jnp.float32)
    latent_single = latents.astype(jnp.float32)
    scores = jnp.einsum('rhl,rpl->rhp', query_f, latent_single) * score_scale
    position = jnp.arange(CACHE_POSITIONS, dtype=jnp.int32)
    valid_key = position[None, None, :] < row_lengths.astype(jnp.int32)[:, None, None]
    valid_key = jnp.broadcast_to(valid_key, scores.shape)
    scores = jnp.where(valid_key, scores, NEG_FILL)
    block_scores = scores.reshape(row_number, ATTENTION_HEADS, N_CTX, CONTEXT_PER_PART)
    block_valid = valid_key.reshape(row_number, ATTENTION_HEADS, N_CTX, CONTEXT_PER_PART)
    block_peak = lax.optimization_barrier(jnp.max(block_scores, axis=-1))
    block_likelihood = jnp.where(block_valid, jnp.exp(block_scores - block_peak[..., None]), 0.0).astype(jnp.bfloat16)
    block_likelihood = lax.optimization_barrier(block_likelihood).astype(jnp.float32)
    block_mass = lax.optimization_barrier(jnp.sum(block_likelihood, axis=-1))
    block_total = jnp.einsum('fsvu,fvuc->fsvc', block_likelihood, latent_single.reshape(row_number, N_CTX, CONTEXT_PER_PART, LATENT_WIDTH))
    fresh_f = fresh.astype(jnp.float32)
    fresh_score = jnp.einsum('rhl,rl->rh', query_f, fresh_f) * score_scale
    new_peak = jnp.maximum(lax.optimization_barrier(jnp.max(block_peak, axis=-1)), fresh_score)
    block_factor = jnp.exp(block_peak - new_peak[..., None])
    fresh_weight = jnp.exp(fresh_score - new_peak).astype(jnp.bfloat16)
    fresh_weight = lax.optimization_barrier(fresh_weight).astype(jnp.float32)
    mass_sum = lax.optimization_barrier(jnp.sum(block_mass * block_factor, axis=-1)) + fresh_weight
    blend_sum = lax.optimization_barrier(jnp.sum(block_total * block_factor[..., None], axis=2)) + fresh_weight[..., None] * fresh_f[:, None, :]
    latent_out = (blend_sum / mass_sum[..., None]).astype(jnp.bfloat16)
    head_values = jnp.einsum('rhl,hlv->rhv', latent_out.astype(jnp.float32), value_up_weight.astype(jnp.float32))
    head_values = head_values.astype(jnp.bfloat16).reshape(row_number, ATTENTION_HEADS * VALUE_WIDTH)
    attention = jnp.dot(head_values, out_proj, preferred_element_type=jnp.float32)
    hidden = residual_rows.astype(jnp.float32) + attention
    inverse = lax.rsqrt(lax.optimization_barrier(jnp.mean(hidden * hidden, axis=-1, keepdims=True)) + EPSILON)
    normed = (hidden * inverse * norm_gain.astype(jnp.float32)).astype(jnp.bfloat16)
    logits = jnp.dot(normed, router, preferred_element_type=jnp.float32)
    chosen = jnp.take_along_axis(logits, picks.astype(jnp.int32), axis=1)
    gate_score = jax.nn.sigmoid(chosen)
    route_weight = (ROUTE_SCALE * gate_score / lax.optimization_barrier(jnp.sum(gate_score, axis=-1, keepdims=True))).astype(jnp.bfloat16)
    shared_mid = jnp.einsum('rd,gdf->grf', normed.astype(jnp.float32), shared_gate_up.astype(jnp.float32))
    shared_act = (jax.nn.silu(shared_mid[0]) * shared_mid[1]).astype(jnp.bfloat16)
    shared_out = jnp.dot(shared_act, shared_down, preferred_element_type=jnp.float32)
    return (hidden, normed, route_weight, shared_out)

def reference(queries, latent_cache, token_latent, lengths, value_up_weight, out_proj, residual, norm_gain, router, expert_ids, expert_gate_up, expert_down, shared_gate_up, shared_down):

    def per_group(group_args):
        return attend_group(group_args, value_up_weight, out_proj, norm_gain, router, shared_gate_up, shared_down)
    hidden, normed, route_weight, shared_out = lax.map(per_group, (queries, latent_cache, lengths, token_latent, residual, expert_ids))
    hidden = hidden.reshape(ROWS, D)
    normed = normed.reshape(ROWS, D)
    route_weight = route_weight.reshape(ROWS, TOPK)
    shared_out = shared_out.reshape(ROWS, D)
    picks = expert_ids.reshape(ROWS * TOPK).astype(jnp.int32)
    order = jnp.argsort(picks, stable=True).astype(jnp.int32)
    expert_range = jnp.arange(EXPERTS, dtype=jnp.int32)
    counts = lax.optimization_barrier(jnp.sum((picks[None, :] == expert_range[:, None]).astype(jnp.int32), axis=1)).astype(jnp.int32)
    starts = (jnp.cumsum(counts) - counts).astype(jnp.int32)
    slot_span = CAP
    order_pad = jnp.concatenate([order, jnp.zeros((slot_span,), jnp.int32)])

    def run_expert(index_value):
        pair_index = lax.dynamic_slice(order_pad, (starts[index_value].astype(jnp.int32),), (slot_span,))
        live = jnp.arange(slot_span, dtype=jnp.int32) < counts[index_value]
        rows_in = normed[pair_index // TOPK]
        middle = jnp.dot(rows_in, expert_gate_up[index_value], preferred_element_type=jnp.float32)
        active = (jax.nn.silu(middle[:, :MOE_FF]) * middle[:, MOE_FF:]).astype(jnp.bfloat16)
        out_rows = jnp.dot(active, expert_down[index_value], preferred_element_type=jnp.float32).astype(jnp.bfloat16)
        target = jnp.where(live, pair_index, ROWS * TOPK).astype(jnp.int32)
        return (out_rows, target)
    expert_rows, targets = lax.map(run_expert, expert_range)
    pair_out = jnp.zeros((ROWS * TOPK + 1, D), jnp.bfloat16).at[targets.reshape(-1)].set(expert_rows.reshape(-1, D))
    pair_out = pair_out[:ROWS * TOPK].reshape(ROWS, TOPK, D)
    routed = lax.optimization_barrier(jnp.sum(route_weight.astype(jnp.float32)[..., None] * pair_out.astype(jnp.float32), axis=1))
    layer_out = (hidden + shared_out + routed).astype(jnp.bfloat16)
    return layer_out.reshape(N_BATCH, ROWS_PER_BATCH, D)
```

```python
import jax
import jax.numpy as jnp
from jax import lax
from jax.sharding import PartitionSpec as P

QK = 192


NEG_FILL = -1e30
ROUTE_SCALE = 2.446
EPSILON = 1e-06


def spread(part, axis):
    copies = jnp.broadcast_to(part[None], (lax.axis_size(axis),) + part.shape)
    return lax.all_to_all(copies, axis, 0, 0)


def local(
    queries,
    latent_cache,
    token_latent,
    lengths,
    value_up_weight,
    out_proj,
    residual,
    norm_gain,
    router,
    expert_ids,
    expert_gate_up,
    expert_down,
    shared_gate_up,
    shared_down,
):
    ctx_index = lax.axis_index("ctx")
    ctx_count = lax.axis_size("ctx")
    batch_count = lax.axis_size("batch")
    batch_index = lax.axis_index("batch")
    own_query = queries[0]
    row_number, heads_here, latent_width = own_query.shape
    score_scale = QK ** (-0.5)
    cache = latent_cache[0]
    span = cache.shape[1]

    every_query = spread(own_query, "ctx").transpose(1, 0, 2, 3)
    every_query = every_query.reshape(row_number, ctx_count * heads_here, latent_width)
    scores = (
        jnp.einsum("rhl,rpl->rhp", every_query, cache, preferred_element_type=jnp.float32)
        * score_scale
    )
    position = ctx_index * span + jnp.arange(span, dtype=jnp.int32)
    valid_key = position[None, None, :] < lengths[0][:, None, None]
    scores = jnp.where(valid_key, scores, NEG_FILL)
    peak = jnp.max(scores, axis=-1, keepdims=True)
    prob = jnp.where(valid_key, jnp.exp(scores - peak), 0.0).astype(jnp.bfloat16)
    mass = jnp.sum(prob.astype(jnp.float32), axis=-1, keepdims=True)
    blend = jnp.einsum("rhp,rpl->rhl", prob, cache, preferred_element_type=jnp.float32)

    pad = jnp.zeros((row_number, ctx_count * heads_here, 126), jnp.float32)
    packed = jnp.concatenate([blend, peak, mass, pad], axis=-1)
    packed = packed.reshape(row_number, ctx_count, heads_here, -1).transpose(1, 0, 2, 3)
    packed = lax.all_to_all(packed, "ctx", 0, 0)
    blends = packed[..., :latent_width]
    peaks = packed[..., latent_width]
    masses = packed[..., latent_width + 1]
    fresh = token_latent[0]
    fresh_score = (
        jnp.einsum("rhl,rl->rh", own_query, fresh, preferred_element_type=jnp.float32) * score_scale
    )
    top = jnp.maximum(jnp.max(peaks, axis=0), fresh_score)
    factors = jnp.exp(peaks - top[None])
    fresh_weight = jnp.exp(fresh_score - top).astype(jnp.bfloat16).astype(jnp.float32)
    mass_sum = jnp.sum(masses * factors, axis=0) + fresh_weight
    blend_sum = (
        jnp.sum(blends * factors[..., None], axis=0)
        + fresh_weight[..., None] * fresh.astype(jnp.float32)[:, None, :]
    )
    latent_out = (blend_sum / mass_sum[..., None]).astype(jnp.bfloat16)
    head_values = jnp.einsum(
        "rhl,hlv->rhv", latent_out, value_up_weight, preferred_element_type=jnp.float32
    )
    head_values = head_values.astype(jnp.bfloat16).reshape(row_number, -1)
    terms = spread(jnp.dot(head_values, out_proj, preferred_element_type=jnp.float32), "ctx")
    hidden = residual[0].astype(jnp.float32) + jnp.sum(terms, axis=0)
    inverse = lax.rsqrt(jnp.mean(hidden * hidden, axis=-1, keepdims=True) + EPSILON)
    normed = (hidden * inverse * norm_gain.astype(jnp.float32)).astype(jnp.bfloat16)

    every_rows = spread(normed, "batch").reshape(batch_count * row_number, -1)
    total_rows = every_rows.shape[0]
    experts_total = router.shape[1]
    all_picks = expert_ids.reshape(total_rows, -1)
    expert_range = jnp.arange(experts_total, dtype=jnp.int32)
    picked = jnp.any(all_picks[:, :, None] == expert_range[None, None, :], axis=1)
    own_expert = ctx_index * batch_count + batch_index
    logits = jnp.dot(every_rows, router, preferred_element_type=jnp.float32)
    gate_score = jnp.where(picked, jax.nn.sigmoid(logits), 0.0)
    own_score = jnp.sum(
        jnp.where(expert_range[None, :] == own_expert, gate_score, 0.0), axis=-1, keepdims=True
    )
    own_weight = (
        (ROUTE_SCALE * own_score / jnp.sum(gate_score, axis=-1, keepdims=True))
        .astype(jnp.bfloat16)
        .astype(jnp.float32)
    )
    expert_width = expert_down.shape[1]
    middle = jnp.dot(every_rows, expert_gate_up[0], preferred_element_type=jnp.float32)
    active = (jax.nn.silu(middle[:, :expert_width]) * middle[:, expert_width:]).astype(jnp.bfloat16)
    answer = jnp.dot(active, expert_down[0], preferred_element_type=jnp.float32).astype(
        jnp.bfloat16
    )
    weighted = (own_weight * answer.astype(jnp.float32)).astype(jnp.bfloat16)

    weighted = weighted.reshape(batch_count, row_number, -1)
    routed = jnp.sum(lax.all_to_all(weighted, "batch", 0, 0).astype(jnp.float32), axis=0)

    shared_mid = jnp.einsum(
        "rd,gdf->grf", normed, shared_gate_up, preferred_element_type=jnp.float32
    )
    shared_act = (jax.nn.silu(shared_mid[0]) * shared_mid[1]).astype(jnp.bfloat16)
    shared_part = jnp.dot(shared_act, shared_down, preferred_element_type=jnp.float32)
    result = hidden + jnp.sum(spread(routed + shared_part, "ctx"), axis=0)
    return result.astype(jnp.bfloat16)[None]


def solution(mesh):
    return jax.shard_map(
        local,
        mesh=mesh,
        in_specs=(
            P("batch", None, "ctx", None),
            P("batch", None, "ctx", None),
            P("batch", None, None),
            P("batch", None),
            P("ctx", None, None),
            P("ctx", None),
            P("batch", None, None),
            P(),
            P(),
            P(),
            P(("ctx", "batch"), None, None),
            P(("ctx", "batch"), None, None),
            P(None, None, "ctx"),
            P("ctx", None),
        ),
        out_specs=P("batch", None, None),
        check_vma=False,
    )
```

```python
import jax
import jax.numpy as jnp
from jax import lax
from jax.experimental import pallas as pl
from jax.experimental.pallas import tpu as pltpu
from jax.sharding import PartitionSpec as P

QK = 192
NEG_FILL = -1e30
ROUTE_SCALE = 2.446
EPSILON = 1e-06
SCALE = QK ** (-0.5)
BF16, F32 = jnp.bfloat16, jnp.float32
VMEM = pl.BlockSpec(memory_space=pltpu.VMEM)
SMEM = pl.BlockSpec(memory_space=pltpu.SMEM)


def call(kernel, out_shape, args, specs=None, limit=16 << 20, scratch=(), cost=None):
    return pl.pallas_call(
        kernel,
        out_shape=out_shape,
        in_specs=specs or [VMEM] * len(args),
        out_specs=jax.tree.map(lambda _: VMEM, out_shape),
        scratch_shapes=list(scratch),
        compiler_params=pltpu.CompilerParams(vmem_limit_bytes=limit),
        cost_estimate=cost,
    )(*args)


def attend_kernel(span_ref, q_ref, cache_ref, out_ref):
    rows, span, width = cache_ref.shape
    parts = q_ref.shape[0]
    heads = q_ref.shape[1] // rows
    every = q_ref[...].astype(F32)
    for r in range(rows):
        own = slice(r * heads, (r + 1) * heads)
        q = every[:, own, :].reshape(parts * heads, width).astype(BF16)
        scores = lax.dot_general(
            q, cache_ref[r], (((1,), (1,)), ((), ())), preferred_element_type=F32
        )
        scores = scores * SCALE
        position = span_ref[rows] + lax.broadcasted_iota(jnp.int32, scores.shape, 1)
        valid = position < span_ref[r]
        scores = jnp.where(valid, scores, NEG_FILL)
        peak = jnp.max(scores, axis=-1, keepdims=True)
        prob = jnp.where(valid, jnp.exp(scores - peak), 0.0).astype(BF16)
        mass = jnp.sum(prob.astype(F32), axis=-1, keepdims=True)
        blend = jnp.dot(prob, cache_ref[r], preferred_element_type=F32)
        lane = lax.broadcasted_iota(jnp.int32, (parts * heads, 128), 1)
        tail = jnp.where(lane == 0, peak, jnp.where(lane == 1, mass, 0.0))
        out_ref[:, own, :width] = blend.reshape(parts, heads, width)
        out_ref[:, own, width:] = tail.reshape(parts, heads, 128)


def project_kernel(parts_ref, q_ref, token_ref, up_ref, proj_ref, out_ref):
    heads, width, _ = up_ref.shape
    rows = token_ref.shape[0]
    token = token_ref[...].astype(F32)
    token = jnp.concatenate(
        [jnp.broadcast_to(token[r : r + 1], (heads, width)) for r in range(rows)], axis=0
    )
    fresh = jnp.sum(q_ref[...].astype(F32) * token, axis=-1, keepdims=True) * SCALE
    peaks = parts_ref[:, :, width : width + 1]
    masses = parts_ref[:, :, width + 1 : width + 2]
    top = jnp.maximum(jnp.max(peaks, axis=0), fresh)
    factors = jnp.exp(peaks - top[None])
    fresh_weight = jnp.exp(fresh - top).astype(BF16).astype(F32)
    mass = jnp.sum(masses * factors, axis=0) + fresh_weight
    blend = jnp.sum(parts_ref[:, :, :width] * factors, axis=0) + fresh_weight * token
    latent = (blend / mass).astype(BF16)
    head = lax.rem(
        lax.broadcasted_iota(jnp.int32, (rows * heads, up_ref.shape[2]), 0), jnp.int32(heads)
    )
    values = [
        jnp.where(head == h, jnp.dot(latent, up_ref[h], preferred_element_type=F32), 0.0).astype(
            BF16
        )
        for h in range(heads)
    ]
    values = jnp.concatenate(values, axis=1)
    step = 256
    for n in range(0, proj_ref.shape[1], step):
        terms = jnp.dot(values, proj_ref[:, n : n + step], preferred_element_type=F32)
        sums = [
            jnp.sum(terms[r * heads : (r + 1) * heads], axis=0, keepdims=True) for r in range(rows)
        ]
        sums = jnp.concatenate(sums, axis=0)
        for c in range(out_ref.shape[0]):
            out_ref[c, :, n : n + step] = sums


def norm_kernel(terms_ref, residual_ref, gain_ref, hidden_ref, normed_ref, copies_ref):
    hidden = residual_ref[...].astype(F32) + jnp.sum(terms_ref[...], axis=0)
    inverse = lax.rsqrt(jnp.mean(hidden * hidden, axis=-1, keepdims=True) + EPSILON)
    normed = (hidden * inverse * gain_ref[...].astype(F32)).astype(BF16)
    hidden_ref[...] = hidden
    normed_ref[...] = normed
    for b in range(copies_ref.shape[0]):
        copies_ref[b] = normed


def expert_kernel(own_ref, rows_ref, picked_ref, router_ref, gate_up_ref, down_ref, out_ref, act):
    rows = rows_ref[...]
    count = rows.shape[0]
    group = out_ref.shape[1]
    width, model = down_ref.shape
    logits = jnp.dot(rows, router_ref[...], preferred_element_type=F32)
    score = jnp.where(picked_ref[...] > 0, jax.nn.sigmoid(logits), 0.0)
    expert = lax.broadcasted_iota(jnp.int32, score.shape, 1)
    own = jnp.sum(jnp.where(expert == own_ref[0], score, 0.0), axis=-1, keepdims=True)
    weight = (ROUTE_SCALE * own / jnp.sum(score, axis=-1, keepdims=True)).astype(BF16).astype(F32)
    step = 256
    for n in range(0, width, step):
        gate = jnp.dot(rows, gate_up_ref[:, n : n + step], preferred_element_type=F32)
        up = jnp.dot(rows, gate_up_ref[:, width + n : width + n + step], preferred_element_type=F32)
        act[:, n : n + step] = (jax.nn.silu(gate) * up).astype(BF16)
    for n in range(0, model, step):
        answer = jnp.dot(act[...], down_ref[:, n : n + step], preferred_element_type=F32)
        answer = weight * answer.astype(BF16).astype(F32)
        out_ref[:, :, n : n + step] = answer.reshape(count // group, group, step).astype(BF16)


def gather_sum_kernel(parts_ref, shared_ref, out_ref):
    total = jnp.sum(parts_ref[...].astype(F32), axis=0) + shared_ref[...]
    for c in range(out_ref.shape[0]):
        out_ref[c] = total


def final_kernel(hidden_ref, terms_ref, out_ref):
    out_ref[...] = (hidden_ref[...] + jnp.sum(terms_ref[...], axis=0)).astype(BF16)


def spread(part, axis):
    copies = jnp.broadcast_to(part[None], (lax.axis_size(axis),) + part.shape)
    return lax.all_to_all(copies, axis, 0, 0)


def local(
    queries,
    latent_cache,
    token_latent,
    lengths,
    value_up_weight,
    out_proj,
    residual,
    norm_gain,
    router,
    expert_ids,
    expert_gate_up,
    expert_down,
    shared_gate_up,
    shared_down,
):
    ctx_index = lax.axis_index("ctx")
    ctx_count = lax.axis_size("ctx")
    batch_count = lax.axis_size("batch")
    batch_index = lax.axis_index("batch")
    _, rows, heads, width = queries.shape
    model = residual.shape[-1]
    experts = router.shape[1]
    total_rows = batch_count * rows
    shape = jax.ShapeDtypeStruct

    own_query = queries.reshape(rows * heads, width)
    every_query = spread(own_query, "ctx")
    start = (ctx_index * latent_cache.shape[2]).astype(jnp.int32)
    span = jnp.concatenate([lengths[0], start[None]])
    parts = call(
        attend_kernel,
        shape((ctx_count, rows * heads, width + 128), F32),
        [span, every_query, latent_cache[0]],
        [SMEM, VMEM, VMEM],
    )
    parts = lax.all_to_all(parts, "ctx", 0, 0)
    terms = call(
        project_kernel,
        shape((ctx_count, rows, model), F32),
        [parts, own_query, token_latent[0], value_up_weight, out_proj],
    )
    terms = lax.all_to_all(terms, "ctx", 0, 0)
    hidden, normed, copies = call(
        norm_kernel,
        (
            shape((rows, model), F32),
            shape((rows, model), BF16),
            shape((batch_count, rows, model), BF16),
        ),
        [terms, residual[0], norm_gain[None]],
    )

    every_rows = lax.all_to_all(copies, "batch", 0, 0).reshape(total_rows, model)
    all_picks = expert_ids.reshape(total_rows, -1)
    expert_range = jnp.arange(experts, dtype=jnp.int32)
    picked = jnp.any(all_picks[:, :, None] == expert_range[None, None, :], axis=1).astype(F32)
    own_expert = (ctx_index * batch_count + batch_index).astype(jnp.int32)[None]
    weighted = call(
        expert_kernel,
        shape((batch_count, rows, model), BF16),
        [own_expert, every_rows, picked, router, expert_gate_up[0], expert_down[0]],
        [SMEM] + [VMEM] * 5,
        scratch=[pltpu.VMEM((total_rows, expert_down.shape[1]), BF16)],
    )
    weighted = lax.all_to_all(weighted, "batch", 0, 0)
    shared_mid = jnp.einsum("rd,gdf->grf", normed, shared_gate_up, preferred_element_type=F32)
    shared_act = (jax.nn.silu(shared_mid[0]) * shared_mid[1]).astype(BF16)
    shared_part = jnp.dot(shared_act, shared_down, preferred_element_type=F32)
    totals = call(
        gather_sum_kernel, shape((ctx_count, rows, model), F32), [weighted, shared_part]
    )
    totals = lax.all_to_all(totals, "ctx", 0, 0)
    return call(final_kernel, shape((rows, model), BF16), [hidden, totals])[None]


def solution(mesh):
    return jax.shard_map(
        local,
        mesh=mesh,
        in_specs=(
            P("batch", None, "ctx", None),
            P("batch", None, "ctx", None),
            P("batch", None, None),
            P("batch", None),
            P("ctx", None, None),
            P("ctx", None),
            P("batch", None, None),
            P(),
            P(),
            P(),
            P(("ctx", "batch"), None, None),
            P(("ctx", "batch"), None, None),
            P(None, None, "ctx"),
            P("ctx", None),
        ),
        out_specs=P("batch", None, None),
        check_vma=False,
    )
```

```python
import jax
import jax.numpy as jnp
from jax import lax
from jax.experimental import pallas as pl
from jax.experimental.pallas import tpu as pltpu
from jax.sharding import PartitionSpec as P

QK = 192
NEG_FILL = -1e30
ROUTE_SCALE = 2.446
EPSILON = 1e-06
SCALE = QK ** (-0.5)
LIMIT = 8 << 20
BF16, F32 = jnp.bfloat16, jnp.float32
VMEM = pl.BlockSpec(memory_space=pltpu.VMEM)
HBM = pl.BlockSpec(memory_space=pltpu.HBM)
SMEM = pl.BlockSpec(memory_space=pltpu.SMEM)


def call(kernel, out_shape, args, specs=None, limit=LIMIT, scratch=(), beside=()):
    beside = [pltpu.with_memory_space_constraint(array, pltpu.HBM) for array in beside]
    count = len(args)

    def body(*refs):
        kernel(*refs[:count], *refs[count + len(beside) :])

    return pl.pallas_call(
        body,
        out_shape=out_shape,
        in_specs=(specs or [VMEM] * count) + [HBM] * len(beside),
        out_specs=jax.tree.map(lambda _: VMEM, out_shape),
        scratch_shapes=list(scratch),
        compiler_params=pltpu.CompilerParams(vmem_limit_bytes=limit),
    )(*args, *beside)


def copies_kernel(part_ref, out_ref):
    for c in range(out_ref.shape[0]):
        out_ref[c] = part_ref[...]


def attend_kernel(span_ref, q_ref, cache_ref, picked_ref, out_ref, kept_ref):
    kept_ref[...] = picked_ref[...]
    rows, span, width = cache_ref.shape
    parts = q_ref.shape[0]
    heads = q_ref.shape[1] // rows
    every = q_ref[...].astype(F32)
    for r in range(rows):
        own = slice(r * heads, (r + 1) * heads)
        q = every[:, own, :].reshape(parts * heads, width).astype(BF16)
        scores = lax.dot_general(
            q, cache_ref[r], (((1,), (1,)), ((), ())), preferred_element_type=F32
        )
        scores = scores * SCALE
        position = span_ref[rows] + lax.broadcasted_iota(jnp.int32, scores.shape, 1)
        valid = position < span_ref[r]
        scores = jnp.where(valid, scores, NEG_FILL)
        peak = jnp.max(scores, axis=-1, keepdims=True)
        prob = jnp.where(valid, jnp.exp(scores - peak), 0.0).astype(BF16)
        mass = jnp.sum(prob.astype(F32), axis=-1, keepdims=True)
        blend = jnp.dot(prob, cache_ref[r], preferred_element_type=F32)
        lane = lax.broadcasted_iota(jnp.int32, (parts * heads, 128), 1)
        tail = jnp.where(lane == 0, peak, jnp.where(lane == 1, mass, 0.0))
        out_ref[:, own, :width] = blend.reshape(parts, heads, width)
        out_ref[:, own, width:] = tail.reshape(parts, heads, 128)


def project_kernel(parts_ref, q_ref, token_ref, up_ref, proj_ref, out_ref):
    heads, width, _ = up_ref.shape
    rows = token_ref.shape[0]
    token = token_ref[...].astype(F32)
    token = jnp.concatenate(
        [jnp.broadcast_to(token[r : r + 1], (heads, width)) for r in range(rows)], axis=0
    )
    fresh = jnp.sum(q_ref[...].astype(F32) * token, axis=-1, keepdims=True) * SCALE
    peaks = parts_ref[:, :, width : width + 1]
    masses = parts_ref[:, :, width + 1 : width + 2]
    top = jnp.maximum(jnp.max(peaks, axis=0), fresh)
    factors = jnp.exp(peaks - top[None])
    fresh_weight = jnp.exp(fresh - top).astype(BF16).astype(F32)
    mass = jnp.sum(masses * factors, axis=0) + fresh_weight
    blend = jnp.sum(parts_ref[:, :, :width] * factors, axis=0) + fresh_weight * token
    latent = (blend / mass).astype(BF16)
    head = lax.rem(
        lax.broadcasted_iota(jnp.int32, (rows * heads, up_ref.shape[2]), 0), jnp.int32(heads)
    )
    values = [
        jnp.where(head == h, jnp.dot(latent, up_ref[h], preferred_element_type=F32), 0.0).astype(
            BF16
        )
        for h in range(heads)
    ]
    values = jnp.concatenate(values, axis=1)
    step = 256
    for n in range(0, proj_ref.shape[1], step):
        terms = jnp.dot(values, proj_ref[:, n : n + step], preferred_element_type=F32)
        sums = [
            jnp.sum(terms[r * heads : (r + 1) * heads], axis=0, keepdims=True) for r in range(rows)
        ]
        sums = jnp.concatenate(sums, axis=0)
        for c in range(out_ref.shape[0]):
            out_ref[c, :, n : n + step] = sums


def norm_kernel(terms_ref, residual_ref, gain_ref, hidden_ref, normed_ref, copies_ref):
    hidden = residual_ref[...].astype(F32) + jnp.sum(terms_ref[...], axis=0)
    inverse = lax.rsqrt(jnp.mean(hidden * hidden, axis=-1, keepdims=True) + EPSILON)
    normed = (hidden * inverse * gain_ref[...].astype(F32)[None]).astype(BF16)
    hidden_ref[...] = hidden
    normed_ref[...] = normed
    for b in range(copies_ref.shape[0]):
        copies_ref[b] = normed


def expert_kernel(own_ref, rows_ref, picked_ref, router_ref, gate_up_ref, down_ref, out_ref, act):
    count = act.shape[0]
    rows = rows_ref[...].astype(F32).reshape(count, rows_ref.shape[2]).astype(BF16)
    group = out_ref.shape[1]
    width, model = down_ref.shape
    logits = jnp.dot(rows, router_ref[...], preferred_element_type=F32)
    score = jnp.where(picked_ref[...] > 0, jax.nn.sigmoid(logits), 0.0)
    expert = lax.broadcasted_iota(jnp.int32, score.shape, 1)
    own = jnp.sum(jnp.where(expert == own_ref[own_ref.shape[0] - 1], score, 0.0), axis=-1, keepdims=True)
    weight = (ROUTE_SCALE * own / jnp.sum(score, axis=-1, keepdims=True)).astype(BF16).astype(F32)
    step = 256
    for n in range(0, width, step):
        gate = jnp.dot(rows, gate_up_ref[:, n : n + step], preferred_element_type=F32)
        up = jnp.dot(rows, gate_up_ref[:, width + n : width + n + step], preferred_element_type=F32)
        act[:, n : n + step] = (jax.nn.silu(gate) * up).astype(BF16)
    for n in range(0, model, step):
        answer = jnp.dot(act[...], down_ref[:, n : n + step], preferred_element_type=F32)
        answer = weight * answer.astype(BF16).astype(F32)
        out_ref[:, :, n : n + step] = answer.reshape(count // group, group, step).astype(BF16)


def shared_kernel(normed_ref, gate_up_ref, down_ref, out_ref, gate_up, down, sems):
    first = pltpu.make_async_copy(gate_up_ref, gate_up, sems.at[0])
    second = pltpu.make_async_copy(down_ref, down, sems.at[1])
    first.start()
    second.start()
    rows, model = normed_ref.shape
    normed = jnp.broadcast_to(normed_ref[...].astype(F32)[None], (8 // rows, rows, model))
    normed = normed.reshape(8, model).astype(BF16)
    first.wait()
    gate = jnp.dot(normed, gate_up[0], preferred_element_type=F32)
    up = jnp.dot(normed, gate_up[1], preferred_element_type=F32)
    act = (jax.nn.silu(gate) * up).astype(BF16)
    second.wait()
    out_ref[...] = jnp.dot(act, down[...], preferred_element_type=F32)[:rows]


def gather_sum_kernel(parts_ref, shared_ref, out_ref):
    total = jnp.sum(parts_ref[...].astype(F32), axis=0) + shared_ref[...]
    for c in range(out_ref.shape[0]):
        out_ref[c] = total


def final_kernel(hidden_ref, terms_ref, out_ref):
    out_ref[...] = (hidden_ref[...] + jnp.sum(terms_ref[...], axis=0)).astype(BF16)


def local(
    queries,
    latent_cache,
    token_latent,
    lengths,
    value_up_weight,
    out_proj,
    residual,
    norm_gain,
    router,
    expert_ids,
    expert_gate_up,
    expert_down,
    shared_gate_up,
    shared_down,
):
    ctx_index = lax.axis_index("ctx")
    ctx_count = lax.axis_size("ctx")
    batch_count = lax.axis_size("batch")
    batch_index = lax.axis_index("batch")
    _, rows, heads, width = queries.shape
    model = residual.shape[-1]
    experts = router.shape[1]
    total_rows = batch_count * rows
    shape = jax.ShapeDtypeStruct

    own_query = queries.reshape(rows * heads, width)
    copies = call(
        copies_kernel,
        shape((ctx_count, rows * heads, width), BF16),
        [own_query],
        beside=[expert_down],
    )
    every_query = lax.all_to_all(copies, "ctx", 0, 0)
    start = ctx_index * latent_cache.shape[2]
    own_expert = ctx_index * batch_count + batch_index
    span = jnp.concatenate([lengths[0], jnp.stack([start, own_expert]).astype(jnp.int32)])
    all_picks = expert_ids.reshape(total_rows, -1)
    expert_range = jnp.arange(experts, dtype=jnp.int32)
    picked = jnp.any(all_picks[:, :, None] == expert_range[None, None, :], axis=1).astype(F32)
    parts, picked = call(
        attend_kernel,
        (
            shape((ctx_count, rows * heads, width + 128), F32),
            shape((total_rows, experts), F32),
        ),
        [span, every_query, latent_cache[0], picked],
        [SMEM, VMEM, VMEM, VMEM],
        beside=[expert_gate_up] * 3,
    )
    parts = lax.all_to_all(parts, "ctx", 0, 0)
    terms = call(
        project_kernel,
        shape((ctx_count, rows, model), F32),
        [parts, own_query, token_latent[0], value_up_weight, out_proj],
    )
    terms = lax.all_to_all(terms, "ctx", 0, 0)
    hidden, normed, copies = call(
        norm_kernel,
        (
            shape((rows, model), F32),
            shape((rows, model), BF16),
            shape((batch_count, rows, model), BF16),
        ),
        [terms, residual[0], norm_gain],
        beside=[expert_gate_up] * 4,
    )

    every_rows = lax.all_to_all(copies, "batch", 0, 0)
    weighted = call(
        expert_kernel,
        shape((batch_count, rows, model), BF16),
        [span, every_rows, picked, router, expert_gate_up[0], expert_down[0]],
        [SMEM] + [VMEM] * 5,
        scratch=[pltpu.VMEM((total_rows, expert_down.shape[1]), BF16)],
    )
    weighted = lax.all_to_all(weighted, "batch", 0, 0)
    shared_part = call(
        shared_kernel,
        shape((rows, model), F32),
        [
            normed,
            pltpu.with_memory_space_constraint(shared_gate_up, pltpu.HBM),
            pltpu.with_memory_space_constraint(shared_down, pltpu.HBM),
        ],
        [VMEM, HBM, HBM],
        scratch=[
            pltpu.VMEM(shared_gate_up.shape, BF16),
            pltpu.VMEM(shared_down.shape, BF16),
            pltpu.SemaphoreType.DMA((2,)),
        ],
    )
    totals = call(
        gather_sum_kernel, shape((ctx_count, rows, model), F32), [weighted, shared_part]
    )
    totals = lax.all_to_all(totals, "ctx", 0, 0)
    return call(final_kernel, shape((rows, model), BF16), [hidden, totals])[None]


def solution(mesh):
    return jax.shard_map(
        local,
        mesh=mesh,
        in_specs=(
            P("batch", None, "ctx", None),
            P("batch", None, "ctx", None),
            P("batch", None, None),
            P("batch", None),
            P("ctx", None, None),
            P("ctx", None),
            P("batch", None, None),
            P(),
            P(),
            P(),
            P(("ctx", "batch"), None, None),
            P(("ctx", "batch"), None, None),
            P(None, None, "ctx"),
            P("ctx", None),
        ),
        out_specs=P("batch", None, None),
        check_vma=False,
    )
```

```python
import functools

import jax
import jax.numpy as jnp
from jax import lax
from jax.experimental import pallas as pl
from jax.experimental.pallas import tpu as pltpu
from jax.sharding import PartitionSpec as P

QK = 192
NEG_FILL = -1e30
ROUTE_SCALE = 2.446
EPSILON = 1e-06
SCALE = QK ** (-0.5)
LIMIT = 8 << 20
BF16, F32 = jnp.bfloat16, jnp.float32
VMEM = pl.BlockSpec(memory_space=pltpu.VMEM)
HBM = pl.BlockSpec(memory_space=pltpu.HBM)
SMEM = pl.BlockSpec(memory_space=pltpu.SMEM)


def call(kernel, out_shape, args, specs=None, limit=LIMIT, scratch=(), beside=()):
    beside = [pltpu.with_memory_space_constraint(array, pltpu.HBM) for array in beside]
    count = len(args)

    def body(*refs):
        kernel(*refs[:count], *refs[count + len(beside) :])

    return pl.pallas_call(
        body,
        out_shape=out_shape,
        in_specs=(specs or [VMEM] * count) + [HBM] * len(beside),
        out_specs=jax.tree.map(lambda _: VMEM, out_shape),
        scratch_shapes=list(scratch),
        compiler_params=pltpu.CompilerParams(vmem_limit_bytes=limit),
    )(*args, *beside)


def picked_kernel(ids_ref, out_ref):
    group, choices, count = ids_ref.shape
    total, experts = out_ref.shape
    expert = lax.broadcasted_iota(jnp.int32, (experts, count), 0)
    row = lax.broadcasted_iota(jnp.int32, (total, count), 0)
    batch = lax.broadcasted_iota(jnp.int32, (total, count), 1)
    picked = jnp.zeros((total, experts), F32)
    for r in range(group):
        named = jnp.zeros((experts, count), F32)
        for k in range(choices):
            named = jnp.where(ids_ref[r, k : k + 1, :] == expert, 1.0, named)
        place = jnp.where(row == batch * group + r, 1.0, 0.0).astype(BF16)
        picked = picked + lax.dot_general(
            place, named.astype(BF16), (((1,), (1,)), ((), ())), preferred_element_type=F32
        )
    out_ref[...] = picked


def attend_kernel(span_ref, *refs):
    count = (len(refs) - 3) // 2
    q_refs, part_refs = refs[:count], refs[count + 2 : -1]
    cache_ref, picked_ref = refs[count : count + 2]
    refs[-1][...] = picked_ref[...]
    rows, span, width = cache_ref.shape
    heads = q_refs[0].shape[0] // rows
    total = count * heads
    every = [q_ref[...].astype(F32) for q_ref in q_refs]
    scores = []
    for r in range(rows):
        q = jnp.concatenate([q[r * heads : (r + 1) * heads] for q in every], axis=0).astype(BF16)
        scores.append(
            lax.dot_general(
                q, cache_ref[r], (((1,), (1,)), ((), ())), preferred_element_type=F32
            )
        )
    position = span_ref[rows] + lax.broadcasted_iota(jnp.int32, (total, span), 1)
    probs, tails = [], []
    lane = lax.broadcasted_iota(jnp.int32, (total, 128), 1)
    for r in range(rows):
        valid = position < span_ref[r]
        score = jnp.where(valid, scores[r] * SCALE, NEG_FILL)
        peak = jnp.max(score, axis=-1, keepdims=True)
        prob = jnp.where(valid, jnp.exp(score - peak), 0.0).astype(BF16)
        mass = jnp.sum(prob.astype(F32), axis=-1, keepdims=True)
        probs.append(prob)
        tails.append(jnp.where(lane == 0, peak, jnp.where(lane == 1, mass, 0.0)))
    for r in range(rows):
        blend = jnp.dot(probs[r], cache_ref[r], preferred_element_type=F32)
        own = slice(r * heads, (r + 1) * heads)
        for m, part_ref in enumerate(part_refs):
            there = slice(m * heads, (m + 1) * heads)
            part_ref[own, :width] = blend[there]
            part_ref[own, width:] = tails[r][there]


def project_kernel(q_ref, token_ref, up_ref, proj_ref, *refs):
    part_refs, out_ref = refs[:-1], refs[-1]
    heads, width, _ = up_ref.shape
    rows = token_ref.shape[0]
    token = token_ref[...].astype(F32)
    token = jnp.concatenate(
        [jnp.broadcast_to(token[r : r + 1], (heads, width)) for r in range(rows)], axis=0
    )
    fresh = jnp.sum(q_ref[...].astype(F32) * token, axis=-1, keepdims=True) * SCALE
    peaks = [part_ref[:, width : width + 1] for part_ref in part_refs]
    top = functools.reduce(jnp.maximum, peaks, fresh)
    mass = jnp.exp(fresh - top).astype(BF16).astype(F32)
    blend = mass * token
    for peak, part_ref in zip(peaks, part_refs):
        factor = jnp.exp(peak - top)
        mass = mass + part_ref[:, width + 1 : width + 2] * factor
        blend = blend + part_ref[:, :width] * factor
    latent = (blend / mass).astype(BF16)
    head = lax.rem(
        lax.broadcasted_iota(jnp.int32, (rows * heads, up_ref.shape[2]), 0), jnp.int32(heads)
    )
    values = [
        jnp.where(head == h, jnp.dot(latent, up_ref[h], preferred_element_type=F32), 0.0).astype(
            BF16
        )
        for h in range(heads)
    ]
    values = jnp.concatenate(values, axis=1)
    step = 256
    for n in range(0, proj_ref.shape[1], step):
        terms = jnp.dot(values, proj_ref[:, n : n + step], preferred_element_type=F32)
        sums = [
            jnp.sum(terms[r * heads : (r + 1) * heads], axis=0, keepdims=True) for r in range(rows)
        ]
        sums = jnp.concatenate(sums, axis=0)
        out_ref[:, n : n + step] = sums


def norm_kernel(residual_ref, gain_ref, *refs):
    hidden_ref, normed_ref, copies_ref = refs[-3:]
    hidden = residual_ref[...].astype(F32) + sum(ref[...] for ref in refs[:-3])
    inverse = lax.rsqrt(jnp.mean(hidden * hidden, axis=-1, keepdims=True) + EPSILON)
    normed = (hidden * inverse * gain_ref[...].astype(F32)[None]).astype(BF16)
    hidden_ref[...] = hidden
    normed_ref[...] = normed
    for b in range(copies_ref.shape[0]):
        copies_ref[b] = normed


def expert_kernel(own_ref, rows_ref, picked_ref, router_ref, gate_up_ref, down_ref, out_ref, act):
    count = act.shape[0]
    rows = rows_ref[...].astype(F32).reshape(count, rows_ref.shape[2]).astype(BF16)
    group = out_ref.shape[1]
    width, model = down_ref.shape
    logits = jnp.dot(rows, router_ref[...], preferred_element_type=F32)
    score = jnp.where(picked_ref[...] > 0, jax.nn.sigmoid(logits), 0.0)
    expert = lax.broadcasted_iota(jnp.int32, score.shape, 1)
    own = jnp.sum(jnp.where(expert == own_ref[own_ref.shape[0] - 1], score, 0.0), axis=-1, keepdims=True)
    weight = (ROUTE_SCALE * own / jnp.sum(score, axis=-1, keepdims=True)).astype(BF16).astype(F32)
    step = 256
    for n in range(0, width, step):
        gate = jnp.dot(rows, gate_up_ref[:, n : n + step], preferred_element_type=F32)
        up = jnp.dot(rows, gate_up_ref[:, width + n : width + n + step], preferred_element_type=F32)
        act[:, n : n + step] = (jax.nn.silu(gate) * up).astype(BF16)
    for n in range(0, model, step):
        answer = jnp.dot(act[...], down_ref[:, n : n + step], preferred_element_type=F32)
        answer = weight * answer.astype(BF16).astype(F32)
        out_ref[:, :, n : n + step] = answer.reshape(count // group, group, step).astype(BF16)


def shared_kernel(normed_ref, gate_up_ref, down_ref, out_ref, gate_up, down, sems):
    first = pltpu.make_async_copy(gate_up_ref, gate_up, sems.at[0])
    second = pltpu.make_async_copy(down_ref, down, sems.at[1])
    first.start()
    second.start()
    rows, model = normed_ref.shape
    normed = jnp.broadcast_to(normed_ref[...].astype(F32)[None], (8 // rows, rows, model))
    normed = normed.reshape(8, model).astype(BF16)
    first.wait()
    gate = jnp.dot(normed, gate_up[0], preferred_element_type=F32)
    up = jnp.dot(normed, gate_up[1], preferred_element_type=F32)
    act = (jax.nn.silu(gate) * up).astype(BF16)
    second.wait()
    out_ref[...] = jnp.dot(act, down[...], preferred_element_type=F32)[:rows]


def gather_sum_kernel(parts_ref, shared_ref, out_ref):
    total = jnp.sum(parts_ref[...].astype(F32), axis=0) + shared_ref[...]
    out_ref[...] = total


def final_kernel(hidden_ref, *refs):
    refs[-1][...] = (hidden_ref[...] + sum(ref[...] for ref in refs[:-1])).astype(BF16)


def swaps(arrays, axis):
    size = lax.axis_size(axis)
    return [
        lax.ppermute(array, axis, [(place, place ^ m) for place in range(size)])
        for m, array in enumerate(arrays, 1)
    ]


def local(
    queries,
    latent_cache,
    token_latent,
    lengths,
    value_up_weight,
    out_proj,
    residual,
    norm_gain,
    router,
    expert_ids,
    expert_gate_up,
    expert_down,
    shared_gate_up,
    shared_down,
):
    ctx_index = lax.axis_index("ctx")
    ctx_count = lax.axis_size("ctx")
    batch_count = lax.axis_size("batch")
    batch_index = lax.axis_index("batch")
    _, rows, heads, width = queries.shape
    model = residual.shape[-1]
    experts = router.shape[1]
    total_rows = batch_count * rows
    shape = jax.ShapeDtypeStruct

    own_query = queries.reshape(rows * heads, width)
    every_query = [own_query] + swaps([own_query] * (ctx_count - 1), "ctx")
    start = ctx_index * latent_cache.shape[2]
    own_expert = ctx_index * batch_count + batch_index
    span = jnp.concatenate([lengths[0], jnp.stack([start, own_expert]).astype(jnp.int32)])
    picked = call(
        picked_kernel,
        shape((total_rows, experts), F32),
        [expert_ids.transpose(1, 2, 0)],
        beside=[expert_gate_up],
    )
    *parts, picked = call(
        attend_kernel,
        [shape((rows * heads, width + 128), F32)] * ctx_count
        + [shape((total_rows, experts), F32)],
        [span, *every_query, latent_cache[0], picked],
        [SMEM] + [VMEM] * (ctx_count + 2),
        beside=[expert_gate_up] * 3,
    )
    parts = [parts[0]] + swaps(parts[1:], "ctx")
    terms = call(
        project_kernel,
        shape((rows, model), F32),
        [own_query, token_latent[0], value_up_weight, out_proj, *parts],
    )
    terms = [terms] + swaps([terms] * (ctx_count - 1), "ctx")
    hidden, normed, copies = call(
        norm_kernel,
        (
            shape((rows, model), F32),
            shape((rows, model), BF16),
            shape((batch_count, rows, model), BF16),
        ),
        [residual[0], norm_gain, *terms],
        beside=[expert_gate_up] * 4,
    )

    every_rows = lax.all_to_all(copies, "batch", 0, 0)
    weighted = call(
        expert_kernel,
        shape((batch_count, rows, model), BF16),
        [span, every_rows, picked, router, expert_gate_up[0], expert_down[0]],
        [SMEM] + [VMEM] * 5,
        scratch=[pltpu.VMEM((total_rows, expert_down.shape[1]), BF16)],
    )
    weighted = lax.all_to_all(weighted, "batch", 0, 0)
    shared_part = call(
        shared_kernel,
        shape((rows, model), F32),
        [
            normed,
            pltpu.with_memory_space_constraint(shared_gate_up, pltpu.HBM),
            pltpu.with_memory_space_constraint(shared_down, pltpu.HBM),
        ],
        [VMEM, HBM, HBM],
        scratch=[
            pltpu.VMEM(shared_gate_up.shape, BF16),
            pltpu.VMEM(shared_down.shape, BF16),
            pltpu.SemaphoreType.DMA((2,)),
        ],
    )
    totals = call(
        gather_sum_kernel, shape((rows, model), F32), [weighted, shared_part]
    )
    totals = [totals] + swaps([totals] * (ctx_count - 1), "ctx")
    return call(final_kernel, shape((rows, model), BF16), [hidden, *totals])[None]


def solution(mesh):
    return jax.shard_map(
        local,
        mesh=mesh,
        in_specs=(
            P("batch", None, "ctx", None),
            P("batch", None, "ctx", None),
            P("batch", None, None),
            P("batch", None),
            P("ctx", None, None),
            P("ctx", None),
            P("batch", None, None),
            P(),
            P(),
            P(),
            P(("ctx", "batch"), None, None),
            P(("ctx", "batch"), None, None),
            P(None, None, "ctx"),
            P("ctx", None),
        ),
        out_specs=P("batch", None, None),
        check_vma=False,
    )
```

```python
import functools

import jax
import jax.numpy as jnp
from jax import lax
from jax.experimental import pallas as pl
from jax.experimental.pallas import tpu as pltpu
from jax.sharding import PartitionSpec as P

QK = 192
NEG_FILL = -1e30
ROUTE_SCALE = 2.446
EPSILON = 1e-06
SCALE = QK ** (-0.5)
LIMIT = 8 << 20
BF16, F32 = jnp.bfloat16, jnp.float32
VMEM = pl.BlockSpec(memory_space=pltpu.VMEM)
HBM = pl.BlockSpec(memory_space=pltpu.HBM)


def call(kernel, out_shape, args, specs=None, limit=LIMIT, scratch=(), beside=()):
    beside = [pltpu.with_memory_space_constraint(array, pltpu.HBM) for array in beside]
    count = len(args)

    def body(*refs):
        kernel(*refs[:count], *refs[count + len(beside) :])

    return pl.pallas_call(
        body,
        out_shape=out_shape,
        in_specs=(specs or [VMEM] * count) + [HBM] * len(beside),
        out_specs=jax.tree.map(lambda _: VMEM, out_shape),
        scratch_shapes=list(scratch),
        compiler_params=pltpu.CompilerParams(vmem_limit_bytes=limit),
    )(*args, *beside)


def split(value):
    high = value.astype(BF16).astype(F32)
    middle = (value - high).astype(BF16).astype(F32)
    return high, middle, value - high - middle


def tree_sum(refs):
    values = [ref[...].astype(F32) for ref in refs]
    while len(values) > 1:
        values = [a + b for a, b in zip(values[::2], values[1::2])]
    return values[0]


def picked_kernel(ids_ref, out_ref):
    group, choices, count = ids_ref.shape
    total, experts = out_ref.shape
    expert = lax.broadcasted_iota(jnp.int32, (experts, count), 0)
    row = lax.broadcasted_iota(jnp.int32, (total, count), 0)
    batch = lax.broadcasted_iota(jnp.int32, (total, count), 1)
    picked = jnp.zeros((total, experts), F32)
    for r in range(group):
        named = jnp.zeros((experts, count), F32)
        for k in range(choices):
            named = jnp.where(ids_ref[r, k : k + 1, :] == expert, 1.0, named)
        place = jnp.where(row == batch * group + r, 1.0, 0.0).astype(BF16)
        picked = picked + lax.dot_general(
            place, named.astype(BF16), (((1,), (1,)), ((), ())), preferred_element_type=F32
        )
    out_ref[...] = picked


def attend_kernel(marks_ref, *refs):
    count = (len(refs) - 4) // 2
    q_refs, part_refs = refs[:count], refs[count + 3 : -1]
    cache_ref, token_ref, picked_ref = refs[count : count + 3]
    refs[-1][...] = picked_ref[...]
    rows, span, width = cache_ref.shape
    heads = q_refs[0].shape[0] // rows
    total = count * heads
    every = [q_ref[...].astype(F32) for q_ref in q_refs]
    scores = []
    for r in range(rows):
        q = jnp.concatenate([q[r * heads : (r + 1) * heads] for q in every], axis=0).astype(BF16)
        scores.append(
            lax.dot_general(
                q, cache_ref[r], (((1,), (1,)), ((), ())), preferred_element_type=F32
            )
        )
    position = lax.broadcasted_iota(jnp.int32, (total, span), 1)
    probs, tails = [], []
    lane = lax.broadcasted_iota(jnp.int32, (total, 128), 1)
    for r in range(rows):
        valid = position < marks_ref[:, r : r + 1]
        score = jnp.where(valid, scores[r] * SCALE, NEG_FILL)
        peak = jnp.max(score, axis=-1, keepdims=True)
        prob = jnp.where(valid, jnp.exp(score - peak), 0.0).astype(BF16)
        mass = jnp.sum(prob.astype(F32), axis=-1, keepdims=True)
        probs.append(prob)
        tail = jnp.zeros((total, 128), F32)
        for place, piece in enumerate(split(peak) + split(mass)):
            tail = jnp.where(lane == place, piece, tail)
        tails.append(tail)
    blends = [jnp.dot(probs[r], cache_ref[r], preferred_element_type=F32) for r in range(rows)]
    for m, part_ref in enumerate(part_refs):
        there = slice(m * heads, (m + 1) * heads)
        part = jnp.concatenate([blend[there] for blend in blends])
        tail = jnp.concatenate([tail[there] for tail in tails])
        if m == 0:
            token = token_ref[...].astype(F32)
            token = [jnp.broadcast_to(token[r : r + 1], (heads, width)) for r in range(rows)]
            token = jnp.concatenate(token, axis=0)
            fresh = jnp.sum(every[0] * token, axis=-1, keepdims=True) * SCALE
            for place, piece in enumerate(split(fresh), 6):
                tail = jnp.where(lane[: rows * heads] == place, piece, tail)
            part_ref[rows * heads :, :width] = token.astype(BF16)
            part_ref[rows * heads :, width:] = jnp.zeros((rows * heads, 128), BF16)
        part_ref[: rows * heads, :width] = part.astype(BF16)
        part_ref[: rows * heads, width:] = tail.astype(BF16)


def project_kernel(up_ref, proj_ref, *refs):
    part_refs, out_ref = refs[:-1], refs[-1]
    heads, width, _ = up_ref.shape
    rows = out_ref.shape[0]
    count = rows * heads
    token = part_refs[0][count:, :width].astype(F32)
    tails = [part_ref[:count, width:].astype(F32) for part_ref in part_refs]
    peaks = [tail[:, 0:1] + (tail[:, 1:2] + tail[:, 2:3]) for tail in tails]
    masses = [tail[:, 3:4] + (tail[:, 4:5] + tail[:, 5:6]) for tail in tails]
    fresh = tails[0][:, 6:7] + (tails[0][:, 7:8] + tails[0][:, 8:9])
    top = functools.reduce(jnp.maximum, peaks, fresh)
    mass = jnp.exp(fresh - top).astype(BF16).astype(F32)
    blend = mass * token
    for there, peak, part_ref in zip(masses, peaks, part_refs):
        factor = jnp.exp(peak - top)
        mass = mass + there * factor
        blend = blend + part_ref[:count, :width].astype(F32) * factor
    latent = (blend / mass).astype(BF16)
    head = lax.rem(
        lax.broadcasted_iota(jnp.int32, (rows * heads, up_ref.shape[2]), 0), jnp.int32(heads)
    )
    values = [
        jnp.where(head == h, jnp.dot(latent, up_ref[h], preferred_element_type=F32), 0.0).astype(
            BF16
        )
        for h in range(heads)
    ]
    values = jnp.concatenate(values, axis=1)
    step = 256
    for n in range(0, proj_ref.shape[1], step):
        terms = jnp.dot(values, proj_ref[:, n : n + step], preferred_element_type=F32)
        sums = [
            jnp.sum(terms[r * heads : (r + 1) * heads], axis=0, keepdims=True) for r in range(rows)
        ]
        sums = jnp.concatenate(sums, axis=0)
        out_ref[:, n : n + step] = sums.astype(BF16)


def norm_kernel(residual_ref, gain_ref, *refs):
    hidden_ref, copies_ref = refs[-2:]
    hidden = residual_ref[...].astype(F32) + tree_sum(refs[:-2])
    inverse = lax.rsqrt(jnp.mean(hidden * hidden, axis=-1, keepdims=True) + EPSILON)
    normed = (hidden * inverse * gain_ref[...].astype(F32)[None]).astype(BF16)
    hidden_ref[...] = hidden
    for b in range(copies_ref.shape[0]):
        copies_ref[b] = normed


def expert_kernel(marks_ref, rows_ref, picked_ref, router_ref, gate_up_ref, down_ref, out_ref, act):
    count = act.shape[0]
    rows = rows_ref[...].astype(F32).reshape(count, rows_ref.shape[2]).astype(BF16)
    pairs, cores, group, _ = out_ref.shape
    width, model = down_ref.shape
    logits = jnp.dot(rows, router_ref[...], preferred_element_type=F32)
    score = jnp.where(picked_ref[...] > 0, jax.nn.sigmoid(logits), 0.0)
    expert = lax.broadcasted_iota(jnp.int32, score.shape, 1)
    own = jnp.where(expert == marks_ref[:, group : group + 1], score, 0.0)
    own = jnp.sum(own, axis=-1, keepdims=True)
    weight = (ROUTE_SCALE * own / jnp.sum(score, axis=-1, keepdims=True)).astype(BF16).astype(F32)
    step = 256
    for n in range(0, width, step):
        gate = jnp.dot(rows, gate_up_ref[:, n : n + step], preferred_element_type=F32)
        up = jnp.dot(rows, gate_up_ref[:, width + n : width + n + step], preferred_element_type=F32)
        act[:, n : n + step] = (jax.nn.silu(gate) * up).astype(BF16)
    for n in range(0, model, step):
        answer = jnp.dot(act[...], down_ref[:, n : n + step], preferred_element_type=F32)
        answer = weight * answer.astype(BF16).astype(F32)
        answer = answer.reshape(pairs, cores, group, step).astype(BF16)
        for core in range(cores):
            out_ref[:, core, :, n : n + step] = answer[:, cores - 1 - core]


def shared_kernel(marks_ref, rows_ref, gate_up_ref, down_ref, out_ref, gate_up, down, sems):
    first = pltpu.make_async_copy(gate_up_ref, gate_up, sems.at[0])
    second = pltpu.make_async_copy(down_ref, down, sems.at[1])
    first.start()
    second.start()
    batches, rows, model = rows_ref.shape
    every = rows_ref[...].astype(F32).reshape(batches * rows, model).astype(BF16)
    row = lax.broadcasted_iota(jnp.int32, (8, batches * rows), 0)
    column = lax.broadcasted_iota(jnp.int32, (8, batches * rows), 1)
    first_row = marks_ref[:, rows + 1 : rows + 2]
    chosen = jnp.where((row < rows) & (column == first_row + row), 1.0, 0.0).astype(BF16)
    normed = jnp.dot(chosen, every, preferred_element_type=F32).astype(BF16)
    first.wait()
    gate = jnp.dot(normed, gate_up[0], preferred_element_type=F32)
    up = jnp.dot(normed, gate_up[1], preferred_element_type=F32)
    act = (jax.nn.silu(gate) * up).astype(BF16)
    second.wait()
    out_ref[...] = jnp.dot(act, down[...], preferred_element_type=F32)[:rows]


def gather_sum_kernel(parts_ref, shared_ref, out_ref):
    total = jnp.sum(parts_ref[...].astype(F32), axis=0) + shared_ref[...]
    out_ref[...] = total.astype(BF16)


def final_kernel(hidden_ref, *refs):
    refs[-1][...] = (hidden_ref[...] + tree_sum(refs[:-1])).astype(BF16)


def swaps(arrays):
    size = lax.axis_size("ctx")
    return [
        lax.ppermute(array, "ctx", [(place, place ^ m) for place in range(size)])
        for m, array in enumerate(arrays, 1)
    ]


def crossings(arrays):
    size, count = lax.axis_size("ctx"), lax.axis_size("batch")
    places = [(c, b) for c in range(size) for b in range(count)]
    return [
        lax.ppermute(
            array,
            ("ctx", "batch"),
            [(c * count + b, (c ^ m) * count + (b ^ 1)) for c, b in places],
        )
        for m, array in enumerate(arrays)
    ]


def local(
    queries,
    latent_cache,
    token_latent,
    lengths,
    value_up_weight,
    out_proj,
    residual,
    norm_gain,
    router,
    expert_ids,
    expert_gate_up,
    expert_down,
    shared_gate_up,
    shared_down,
):
    ctx_index = lax.axis_index("ctx")
    ctx_count = lax.axis_size("ctx")
    batch_count = lax.axis_size("batch")
    batch_index = lax.axis_index("batch")
    _, rows, heads, width = queries.shape
    model = residual.shape[-1]
    experts = router.shape[1]
    total_rows = batch_count * rows
    shape = jax.ShapeDtypeStruct

    own_query = queries.reshape(rows * heads, width)
    every_query = [own_query] + swaps([own_query] * (ctx_count - 1))
    valid = lengths - (ctx_index * latent_cache.shape[2]).astype(jnp.int32)
    places = jnp.stack([ctx_index * batch_count + batch_index, (batch_index ^ 1) * rows])
    marks = jnp.concatenate([valid, places.astype(jnp.int32)[None]], axis=1)
    picked = call(
        picked_kernel,
        shape((total_rows, experts), F32),
        [expert_ids.transpose(1, 2, 0)],
        beside=[expert_gate_up],
    )
    *parts, picked = call(
        attend_kernel,
        [shape((2 * rows * heads, width + 128), BF16)]
        + [shape((rows * heads, width + 128), BF16)] * (ctx_count - 1)
        + [shape((total_rows, experts), F32)],
        [marks, *every_query, latent_cache[0], token_latent[0], picked],
        beside=[expert_gate_up] * 3,
    )
    parts = crossings(parts)
    terms = call(
        project_kernel,
        shape((rows, model), BF16),
        [value_up_weight, out_proj, *parts],
    )
    terms = crossings([terms] * ctx_count)
    hidden, copies = call(
        norm_kernel,
        (
            shape((rows, model), F32),
            shape((batch_count, rows, model), BF16),
        ),
        [residual[0], norm_gain, *terms],
        beside=[expert_gate_up] * 4,
    )

    every_rows = lax.all_to_all(copies, "batch", 0, 0)
    weighted = call(
        expert_kernel,
        shape((batch_count // 2, 2, rows, model), BF16),
        [marks, every_rows, picked, router, expert_gate_up[0], expert_down[0]],
        scratch=[pltpu.VMEM((total_rows, expert_down.shape[1]), BF16)],
    )
    weighted = weighted.reshape(batch_count, rows, model)
    weighted = lax.all_to_all(weighted, "batch", 0, 0)
    shared_part = call(
        shared_kernel,
        shape((rows, model), F32),
        [
            marks,
            every_rows,
            pltpu.with_memory_space_constraint(shared_gate_up, pltpu.HBM),
            pltpu.with_memory_space_constraint(shared_down, pltpu.HBM),
        ],
        [VMEM, VMEM, HBM, HBM],
        scratch=[
            pltpu.VMEM(shared_gate_up.shape, BF16),
            pltpu.VMEM(shared_down.shape, BF16),
            pltpu.SemaphoreType.DMA((2,)),
        ],
    )
    totals = call(
        gather_sum_kernel, shape((rows, model), BF16), [weighted, shared_part]
    )
    totals = crossings([totals] * ctx_count)
    return call(final_kernel, shape((rows, model), BF16), [hidden, *totals])[None]


def solution(mesh):
    return jax.shard_map(
        local,
        mesh=mesh,
        in_specs=(
            P("batch", None, "ctx", None),
            P("batch", None, "ctx", None),
            P("batch", None, None),
            P("batch", None),
            P("ctx", None, None),
            P("ctx", None),
            P("batch", None, None),
            P(),
            P(),
            P(),
            P(("ctx", "batch"), None, None),
            P(("ctx", "batch"), None, None),
            P(None, None, "ctx"),
            P("ctx", None),
        ),
        out_specs=P("batch", None, None),
        check_vma=False,
    )
```

```python
import functools

import jax
import jax.numpy as jnp
from jax import lax
from jax.experimental import pallas as pl
from jax.experimental.pallas import tpu as pltpu
from jax.sharding import PartitionSpec as P

QK = 192
NEG_FILL = -1e30
ROUTE_SCALE = 2.446
EPSILON = 1e-06
SCALE = QK ** (-0.5)
LIMIT = 8 << 20
BF16, F32 = jnp.bfloat16, jnp.float32
VMEM = pl.BlockSpec(memory_space=pltpu.VMEM)
HBM = pl.BlockSpec(memory_space=pltpu.HBM)


def call(kernel, out_shape, args, specs=None, limit=LIMIT, scratch=(), beside=()):
    beside = [pltpu.with_memory_space_constraint(array, pltpu.HBM) for array in beside]
    count = len(args)

    def body(*refs):
        kernel(*refs[:count], *refs[count + len(beside) :])

    return pl.pallas_call(
        body,
        out_shape=out_shape,
        in_specs=(specs or [VMEM] * count) + [HBM] * len(beside),
        out_specs=jax.tree.map(lambda _: VMEM, out_shape),
        scratch_shapes=list(scratch),
        compiler_params=pltpu.CompilerParams(vmem_limit_bytes=limit),
    )(*args, *beside)


def split(value):
    high = value.astype(BF16).astype(F32)
    middle = (value - high).astype(BF16).astype(F32)
    return high, middle, value - high - middle


def tree_sum(refs):
    values = [ref[...].astype(F32) for ref in refs]
    while len(values) > 1:
        values = [a + b for a, b in zip(values[::2], values[1::2])]
    return values[0]


def picked_kernel(ids_hbm, lengths_hbm, out_ref, lengths_ref, ids_ref, sems):
    copies = [
        pltpu.make_async_copy(ids_hbm, ids_ref, sems.at[0]),
        pltpu.make_async_copy(lengths_hbm, lengths_ref, sems.at[1]),
    ]
    for copy in copies:
        copy.start()
    for copy in copies:
        copy.wait()
    group, choices, count = ids_ref.shape
    total, experts = out_ref.shape
    expert = lax.broadcasted_iota(jnp.int32, (experts, count), 0)
    row = lax.broadcasted_iota(jnp.int32, (total, count), 0)
    batch = lax.broadcasted_iota(jnp.int32, (total, count), 1)
    picked = jnp.zeros((total, experts), F32)
    for r in range(group):
        named = jnp.zeros((experts, count), F32)
        for k in range(choices):
            named = jnp.where(ids_ref[r, k : k + 1, :] == expert, 1.0, named)
        place = jnp.where(row == batch * group + r, 1.0, 0.0).astype(BF16)
        picked = picked + lax.dot_general(
            place, named.astype(BF16), (((1,), (1,)), ((), ())), preferred_element_type=F32
        )
    out_ref[...] = picked


def attend_kernel(marks_ref, *refs):
    count = (len(refs) - 4) // 2
    q_refs, part_refs = refs[:count], refs[count + 3 : -1]
    cache_ref, token_ref, picked_ref = refs[count : count + 3]
    refs[-1][...] = picked_ref[...]
    rows, span, width = cache_ref.shape
    heads = q_refs[0].shape[0] // rows
    total = count * heads
    every = [q_ref[...].astype(F32) for q_ref in q_refs]
    scores = []
    for r in range(rows):
        q = jnp.concatenate([q[r * heads : (r + 1) * heads] for q in every], axis=0).astype(BF16)
        scores.append(
            lax.dot_general(
                q, cache_ref[r], (((1,), (1,)), ((), ())), preferred_element_type=F32
            )
        )
    position = lax.broadcasted_iota(jnp.int32, (total, span), 1)
    probs, tails = [], []
    lane = lax.broadcasted_iota(jnp.int32, (total, 128), 1)
    for r in range(rows):
        valid = position < marks_ref[:, r : r + 1]
        score = jnp.where(valid, scores[r] * SCALE, NEG_FILL)
        peak = jnp.max(score, axis=-1, keepdims=True)
        prob = jnp.where(valid, jnp.exp(score - peak), 0.0).astype(BF16)
        mass = jnp.sum(prob.astype(F32), axis=-1, keepdims=True)
        probs.append(prob)
        tail = jnp.zeros((total, 128), F32)
        for place, piece in enumerate(split(peak) + split(mass)):
            tail = jnp.where(lane == place, piece, tail)
        tails.append(tail)
    blends = [jnp.dot(probs[r], cache_ref[r], preferred_element_type=F32) for r in range(rows)]
    for m, part_ref in enumerate(part_refs):
        there = slice(m * heads, (m + 1) * heads)
        part = jnp.concatenate([blend[there] for blend in blends])
        tail = jnp.concatenate([tail[there] for tail in tails])
        if m == 0:
            token = token_ref[...].astype(F32)
            token = [jnp.broadcast_to(token[r : r + 1], (heads, width)) for r in range(rows)]
            token = jnp.concatenate(token, axis=0)
            fresh = jnp.sum(every[0] * token, axis=-1, keepdims=True) * SCALE
            for place, piece in enumerate(split(fresh), 6):
                tail = jnp.where(lane[: rows * heads] == place, piece, tail)
            part_ref[rows * heads :, :width] = token.astype(BF16)
            part_ref[rows * heads :, width:] = jnp.zeros((rows * heads, 128), BF16)
        part_ref[: rows * heads, :width] = part.astype(BF16)
        part_ref[: rows * heads, width:] = tail.astype(BF16)


def project_kernel(up_ref, proj_ref, *refs):
    part_refs, out_ref = refs[-2::-1], refs[-1]
    heads, width, _ = up_ref.shape
    rows = out_ref.shape[0]
    count = rows * heads
    token = part_refs[0][count:, :width].astype(F32)
    tails = [part_ref[:count, width:].astype(F32) for part_ref in part_refs]
    peaks = [tail[:, 0:1] + (tail[:, 1:2] + tail[:, 2:3]) for tail in tails]
    masses = [tail[:, 3:4] + (tail[:, 4:5] + tail[:, 5:6]) for tail in tails]
    fresh = tails[0][:, 6:7] + (tails[0][:, 7:8] + tails[0][:, 8:9])
    top = functools.reduce(jnp.maximum, peaks, fresh)
    mass = jnp.exp(fresh - top).astype(BF16).astype(F32)
    blend = mass * token
    for there, peak, part_ref in zip(masses, peaks, part_refs):
        factor = jnp.exp(peak - top)
        mass = mass + there * factor
        blend = blend + part_ref[:count, :width].astype(F32) * factor
    latent = (blend / mass).astype(BF16)
    head = lax.rem(
        lax.broadcasted_iota(jnp.int32, (rows * heads, up_ref.shape[2]), 0), jnp.int32(heads)
    )
    values = [
        jnp.where(head == h, jnp.dot(latent, up_ref[h], preferred_element_type=F32), 0.0).astype(
            BF16
        )
        for h in range(heads)
    ]
    values = jnp.concatenate(values, axis=1)
    step = 256
    for n in range(0, proj_ref.shape[1], step):
        terms = jnp.dot(values, proj_ref[:, n : n + step], preferred_element_type=F32)
        sums = [
            jnp.sum(terms[r * heads : (r + 1) * heads], axis=0, keepdims=True) for r in range(rows)
        ]
        sums = jnp.concatenate(sums, axis=0)
        out_ref[:, n : n + step] = sums.astype(BF16)


def norm_kernel(residual_ref, gain_ref, *refs):
    hidden_ref, copies_ref = refs[-2:]
    hidden = residual_ref[...].astype(F32) + tree_sum(refs[:-2])
    inverse = lax.rsqrt(jnp.mean(hidden * hidden, axis=-1, keepdims=True) + EPSILON)
    normed = (hidden * inverse * gain_ref[...].astype(F32)[None]).astype(BF16)
    hidden_ref[...] = hidden
    for b in range(copies_ref.shape[0]):
        copies_ref[b] = normed


def expert_kernel(
    marks_ref,
    rows_ref,
    picked_ref,
    router_ref,
    gate_up_ref,
    down_ref,
    shared_gate_up_ref,
    shared_down_ref,
    out_ref,
    shared_ref,
    act,
):
    count = act.shape[0]
    rows = rows_ref[...].astype(F32).reshape(count, rows_ref.shape[2]).astype(BF16)
    pairs, cores, group, _ = out_ref.shape
    width, model = down_ref.shape
    logits = jnp.dot(rows, router_ref[...], preferred_element_type=F32)
    score = jnp.where(picked_ref[...] > 0, jax.nn.sigmoid(logits), 0.0)
    expert = lax.broadcasted_iota(jnp.int32, score.shape, 1)
    own = jnp.where(expert == marks_ref[:, group : group + 1], score, 0.0)
    own = jnp.sum(own, axis=-1, keepdims=True)
    weight = (ROUTE_SCALE * own / jnp.sum(score, axis=-1, keepdims=True)).astype(BF16).astype(F32)
    step = 256
    for n in range(0, width, step):
        gate = jnp.dot(rows, gate_up_ref[:, n : n + step], preferred_element_type=F32)
        up = jnp.dot(rows, gate_up_ref[:, width + n : width + n + step], preferred_element_type=F32)
        act[:, n : n + step] = (jax.nn.silu(gate) * up).astype(BF16)
    for n in range(0, model, step):
        answer = jnp.dot(act[...], down_ref[:, n : n + step], preferred_element_type=F32)
        answer = weight * answer.astype(BF16).astype(F32)
        answer = answer.reshape(pairs, cores, group, step).astype(BF16)
        for core in range(cores):
            out_ref[:, core, :, n : n + step] = answer[:, cores - 1 - core]
    row = lax.broadcasted_iota(jnp.int32, (8, count), 0)
    column = lax.broadcasted_iota(jnp.int32, (8, count), 1)
    first_row = marks_ref[:, group + 1 : group + 2]
    chosen = jnp.where((row < group) & (column == first_row + row), 1.0, 0.0).astype(BF16)
    chosen = jnp.dot(chosen, rows, preferred_element_type=F32).astype(BF16)
    gate = jnp.dot(chosen, shared_gate_up_ref[0], preferred_element_type=F32)
    up = jnp.dot(chosen, shared_gate_up_ref[1], preferred_element_type=F32)
    shared = (jax.nn.silu(gate) * up).astype(BF16)
    shared = jnp.dot(shared, shared_down_ref[...], preferred_element_type=F32)
    shared_ref[...] = shared[:group]


def gather_sum_kernel(parts_ref, shared_ref, out_ref):
    total = jnp.sum(parts_ref[...].astype(F32), axis=0) + shared_ref[...]
    out_ref[...] = total.astype(BF16)


def final_kernel(hidden_ref, *refs):
    refs[-1][...] = (hidden_ref[...] + tree_sum(refs[:-1])).astype(BF16)


def offsets():
    return [m ^ (m >> 1) for m in range(lax.axis_size("ctx"))]


def swaps(array):
    size = lax.axis_size("ctx")
    return [
        lax.ppermute(array, "ctx", [(place, place ^ m) for place in range(size)])
        for m in offsets()[1:]
    ]


def crossings(arrays):
    size, count = lax.axis_size("ctx"), lax.axis_size("batch")
    places = [(c, b) for c in range(size) for b in range(count)]
    return [
        lax.ppermute(
            array,
            ("ctx", "batch"),
            [(c * count + b, (c ^ m) * count + (b ^ 1)) for c, b in places],
        )
        for m, array in zip(offsets(), arrays, strict=True)
    ]


def local(
    queries,
    latent_cache,
    token_latent,
    lengths,
    value_up_weight,
    out_proj,
    residual,
    norm_gain,
    router,
    expert_ids,
    expert_gate_up,
    expert_down,
    shared_gate_up,
    shared_down,
):
    ctx_index = lax.axis_index("ctx")
    ctx_count = lax.axis_size("ctx")
    batch_count = lax.axis_size("batch")
    batch_index = lax.axis_index("batch")
    _, rows, heads, width = queries.shape
    model = residual.shape[-1]
    experts = router.shape[1]
    total_rows = batch_count * rows
    shape = jax.ShapeDtypeStruct

    own_query = queries.reshape(rows * heads, width)
    every_query = [own_query] + swaps(own_query)
    ids = expert_ids.transpose(1, 2, 0)
    picked, own_lengths = call(
        picked_kernel,
        (shape((total_rows, experts), F32), shape(lengths.shape, jnp.int32)),
        [
            pltpu.with_memory_space_constraint(ids, pltpu.HBM),
            pltpu.with_memory_space_constraint(lengths, pltpu.HBM),
        ],
        [HBM, HBM],
        scratch=[pltpu.VMEM(ids.shape, jnp.int32), pltpu.SemaphoreType.DMA((2,))],
        beside=[expert_gate_up],
    )
    valid = own_lengths - (ctx_index * latent_cache.shape[2]).astype(jnp.int32)
    places = jnp.stack([ctx_index * batch_count + batch_index, (batch_index ^ 1) * rows])
    marks = jnp.concatenate([valid, places.astype(jnp.int32)[None]], axis=1)
    *parts, picked = call(
        attend_kernel,
        [shape((2 * rows * heads, width + 128), BF16)]
        + [shape((rows * heads, width + 128), BF16)] * (ctx_count - 1)
        + [shape((total_rows, experts), F32)],
        [marks, *every_query, latent_cache[0], token_latent[0], picked],
        beside=[expert_gate_up] * 3,
    )
    parts = crossings(parts)
    terms = call(
        project_kernel,
        shape((rows, model), BF16),
        [value_up_weight, out_proj, *parts[::-1]],
    )
    terms = crossings([terms] * ctx_count)
    hidden, copies = call(
        norm_kernel,
        (
            shape((rows, model), F32),
            shape((batch_count, rows, model), BF16),
        ),
        [residual[0], norm_gain, *terms],
        beside=[expert_gate_up] * 4,
    )

    every_rows = lax.all_to_all(copies, "batch", 0, 0)
    weighted, shared_part = call(
        expert_kernel,
        (
            shape((batch_count // 2, 2, rows, model), BF16),
            shape((rows, model), F32),
        ),
        [
            marks,
            every_rows,
            picked,
            router,
            expert_gate_up[0],
            expert_down[0],
            shared_gate_up,
            shared_down,
        ],
        scratch=[pltpu.VMEM((total_rows, expert_down.shape[1]), BF16)],
    )
    weighted = weighted.reshape(batch_count, rows, model)
    weighted = lax.all_to_all(weighted, "batch", 0, 0)
    totals = call(
        gather_sum_kernel, shape((rows, model), BF16), [weighted, shared_part]
    )
    totals = crossings([totals] * ctx_count)
    return call(final_kernel, shape((rows, model), BF16), [hidden, *totals])[None]


def solution(mesh):
    return jax.shard_map(
        local,
        mesh=mesh,
        in_specs=(
            P("batch", None, "ctx", None),
            P("batch", None, "ctx", None),
            P("batch", None, None),
            P("batch", None),
            P("ctx", None, None),
            P("ctx", None),
            P("batch", None, None),
            P(),
            P(),
            P(),
            P(("ctx", "batch"), None, None),
            P(("ctx", "batch"), None, None),
            P(None, None, "ctx"),
            P("ctx", None),
        ),
        out_specs=P("batch", None, None),
        check_vma=False,
    )
```

```python
import functools

import jax
import jax.numpy as jnp
from jax import lax
from jax.experimental import pallas as pl
from jax.experimental.pallas import tpu as pltpu
from jax.sharding import PartitionSpec as P

QK = 192
NEG_FILL = -1e30
ROUTE_SCALE = 2.446
EPSILON = 1e-06
SCALE = QK ** (-0.5)
LIMIT = 8 << 20
BF16, F32 = jnp.bfloat16, jnp.float32
VMEM = pl.BlockSpec(memory_space=pltpu.VMEM)
HBM = pl.BlockSpec(memory_space=pltpu.HBM)


def call(kernel, out_shape, args, specs=None, limit=LIMIT, scratch=(), beside=()):
    beside = [pltpu.with_memory_space_constraint(array, pltpu.HBM) for array in beside]
    count = len(args)

    def body(*refs):
        kernel(*refs[:count], *refs[count + len(beside) :])

    return pl.pallas_call(
        body,
        out_shape=out_shape,
        in_specs=(specs or [VMEM] * count) + [HBM] * len(beside),
        out_specs=jax.tree.map(lambda _: VMEM, out_shape),
        scratch_shapes=list(scratch),
        compiler_params=pltpu.CompilerParams(vmem_limit_bytes=limit),
    )(*args, *beside)


def split(value):
    high = value.astype(BF16).astype(F32)
    middle = (value - high).astype(BF16).astype(F32)
    return high, middle, value - high - middle


def tree_sum(refs):
    values = [ref[...].astype(F32) for ref in refs]
    while len(values) > 1:
        values = [a + b for a, b in zip(values[::2], values[1::2])]
    return values[0]


def by_heads(token, heads):
    token = token.astype(F32)
    rows, width = token.shape
    token = [jnp.broadcast_to(token[r : r + 1], (heads, width)) for r in range(rows)]
    return jnp.concatenate(token, axis=0)


def picked_kernel(ids_hbm, lengths_hbm, out_ref, lengths_ref, ids_ref, sems):
    copies = [
        pltpu.make_async_copy(ids_hbm, ids_ref, sems.at[0]),
        pltpu.make_async_copy(lengths_hbm, lengths_ref, sems.at[1]),
    ]
    for copy in copies:
        copy.start()
    for copy in copies:
        copy.wait()
    group, choices, count = ids_ref.shape
    total, experts = out_ref.shape
    expert = lax.broadcasted_iota(jnp.int32, (experts, count), 0)
    row = lax.broadcasted_iota(jnp.int32, (total, count), 0)
    batch = lax.broadcasted_iota(jnp.int32, (total, count), 1)
    picked = jnp.zeros((total, experts), F32)
    for r in range(group):
        named = jnp.zeros((experts, count), F32)
        for k in range(choices):
            named = jnp.where(ids_ref[r, k : k + 1, :] == expert, 1.0, named)
        place = jnp.where(row == batch * group + r, 1.0, 0.0).astype(BF16)
        picked = picked + lax.dot_general(
            place, named.astype(BF16), (((1,), (1,)), ((), ())), preferred_element_type=F32
        )
    out_ref[...] = picked


def attend_kernel(marks_ref, *refs):
    count = (len(refs) - 4) // 2
    q_refs, part_refs = refs[:count], refs[count + 3 : -1]
    cache_ref, token_ref, picked_ref = refs[count : count + 3]
    refs[-1][...] = picked_ref[...]
    rows, span, width = cache_ref.shape
    heads = q_refs[0].shape[0] // rows
    total = count * heads
    every = [q_ref[...].astype(F32) for q_ref in q_refs]
    scores = []
    for r in range(rows):
        q = jnp.concatenate([q[r * heads : (r + 1) * heads] for q in every], axis=0).astype(BF16)
        scores.append(
            lax.dot_general(
                q, cache_ref[r], (((1,), (1,)), ((), ())), preferred_element_type=F32
            )
        )
    position = lax.broadcasted_iota(jnp.int32, (total, span), 1)
    probs, tails = [], []
    lane = lax.broadcasted_iota(jnp.int32, (total, 128), 1)
    for r in range(rows):
        valid = position < marks_ref[:, r : r + 1]
        score = jnp.where(valid, scores[r] * SCALE, NEG_FILL)
        peak = jnp.max(score, axis=-1, keepdims=True)
        prob = jnp.where(valid, jnp.exp(score - peak), 0.0).astype(BF16)
        mass = jnp.sum(prob.astype(F32), axis=-1, keepdims=True)
        probs.append(prob)
        tail = jnp.zeros((total, 128), F32)
        for place, piece in enumerate(split(peak) + split(mass)):
            tail = jnp.where(lane == place, piece, tail)
        tails.append(tail)
    blends = [jnp.dot(probs[r], cache_ref[r], preferred_element_type=F32) for r in range(rows)]
    for m, part_ref in enumerate(part_refs):
        there = slice(m * heads, (m + 1) * heads)
        part = jnp.concatenate([blend[there] for blend in blends])
        tail = jnp.concatenate([tail[there] for tail in tails])
        if m == 0:
            token = by_heads(token_ref[...], heads)
            fresh = jnp.sum(every[0] * token, axis=-1, keepdims=True) * SCALE
            for place, piece in enumerate(split(fresh), 6):
                tail = jnp.where(lane[: rows * heads] == place, piece, tail)
        part_ref[:, :width] = part.astype(BF16)
        part_ref[:, width:] = tail.astype(BF16)


def project_kernel(up_ref, proj_ref, token_ref, *refs):
    part_refs, out_ref = refs[-2::-1], refs[-1]
    heads, width, _ = up_ref.shape
    rows = out_ref.shape[0]
    token = by_heads(token_ref[...], heads)
    tails = [part_ref[:, width:].astype(F32) for part_ref in part_refs]
    peaks = [tail[:, 0:1] + (tail[:, 1:2] + tail[:, 2:3]) for tail in tails]
    masses = [tail[:, 3:4] + (tail[:, 4:5] + tail[:, 5:6]) for tail in tails]
    fresh = tails[0][:, 6:7] + (tails[0][:, 7:8] + tails[0][:, 8:9])
    top = functools.reduce(jnp.maximum, peaks, fresh)
    mass = jnp.exp(fresh - top).astype(BF16).astype(F32)
    blend = mass * token
    for there, peak, part_ref in zip(masses, peaks, part_refs):
        factor = jnp.exp(peak - top)
        mass = mass + there * factor
        blend = blend + part_ref[:, :width].astype(F32) * factor
    latent = (blend / mass).astype(BF16)
    head = lax.rem(
        lax.broadcasted_iota(jnp.int32, (rows * heads, up_ref.shape[2]), 0), jnp.int32(heads)
    )
    values = [
        jnp.where(head == h, jnp.dot(latent, up_ref[h], preferred_element_type=F32), 0.0).astype(
            BF16
        )
        for h in range(heads)
    ]
    values = jnp.concatenate(values, axis=1)
    step = 256
    for n in range(0, proj_ref.shape[1], step):
        terms = jnp.dot(values, proj_ref[:, n : n + step], preferred_element_type=F32)
        sums = [
            jnp.sum(terms[r * heads : (r + 1) * heads], axis=0, keepdims=True) for r in range(rows)
        ]
        sums = jnp.concatenate(sums, axis=0)
        out_ref[:, n : n + step] = sums.astype(BF16)


def norm_kernel(residual_ref, gain_ref, *refs):
    hidden_ref, copies_ref = refs[-2:]
    hidden = residual_ref[...].astype(F32) + tree_sum(refs[:-2])
    inverse = lax.rsqrt(jnp.mean(hidden * hidden, axis=-1, keepdims=True) + EPSILON)
    normed = (hidden * inverse * gain_ref[...].astype(F32)[None]).astype(BF16)
    hidden_ref[...] = hidden
    for b in range(copies_ref.shape[0]):
        copies_ref[b] = normed


def expert_kernel(
    marks_ref,
    rows_ref,
    picked_ref,
    router_ref,
    gate_up_ref,
    down_ref,
    shared_gate_up_ref,
    shared_down_ref,
    out_ref,
    shared_ref,
    act,
):
    count = act.shape[0]
    rows = rows_ref[...].astype(F32).reshape(count, rows_ref.shape[2]).astype(BF16)
    pairs, cores, group, _ = out_ref.shape
    width, model = down_ref.shape
    logits = jnp.dot(rows, router_ref[...], preferred_element_type=F32)
    score = jnp.where(picked_ref[...] > 0, jax.nn.sigmoid(logits), 0.0)
    expert = lax.broadcasted_iota(jnp.int32, score.shape, 1)
    own = jnp.where(expert == marks_ref[:, group : group + 1], score, 0.0)
    own = jnp.sum(own, axis=-1, keepdims=True)
    weight = (ROUTE_SCALE * own / jnp.sum(score, axis=-1, keepdims=True)).astype(BF16).astype(F32)
    step = 256
    for n in range(0, width, step):
        gate = jnp.dot(rows, gate_up_ref[:, n : n + step], preferred_element_type=F32)
        up = jnp.dot(rows, gate_up_ref[:, width + n : width + n + step], preferred_element_type=F32)
        act[:, n : n + step] = (jax.nn.silu(gate) * up).astype(BF16)
    for n in range(0, model, step):
        answer = jnp.dot(act[...], down_ref[:, n : n + step], preferred_element_type=F32)
        answer = weight * answer.astype(BF16).astype(F32)
        answer = answer.reshape(pairs, cores, group, step).astype(BF16)
        for core in range(cores):
            out_ref[:, core, :, n : n + step] = answer[:, cores - 1 - core]
    row = lax.broadcasted_iota(jnp.int32, (8, count), 0)
    column = lax.broadcasted_iota(jnp.int32, (8, count), 1)
    first_row = marks_ref[:, group + 1 : group + 2]
    chosen = jnp.where((row < group) & (column == first_row + row), 1.0, 0.0).astype(BF16)
    chosen = jnp.dot(chosen, rows, preferred_element_type=F32).astype(BF16)
    gate = jnp.dot(chosen, shared_gate_up_ref[0], preferred_element_type=F32)
    up = jnp.dot(chosen, shared_gate_up_ref[1], preferred_element_type=F32)
    shared = (jax.nn.silu(gate) * up).astype(BF16)
    shared = jnp.dot(shared, shared_down_ref[...], preferred_element_type=F32)
    shared_ref[...] = shared[:group]


def gather_sum_kernel(parts_ref, shared_ref, out_ref):
    total = jnp.sum(parts_ref[...].astype(F32), axis=0) + shared_ref[...]
    out_ref[...] = total.astype(BF16)


def final_kernel(hidden_ref, *refs):
    refs[-1][...] = (hidden_ref[...] + tree_sum(refs[:-1])).astype(BF16)


def offsets():
    return [m ^ (m >> 1) for m in range(lax.axis_size("ctx"))]


def swaps(array):
    size = lax.axis_size("ctx")
    return [
        lax.ppermute(array, "ctx", [(place, place ^ m) for place in range(size)])
        for m in offsets()[1:]
    ]


def crossings(arrays):
    size, count = lax.axis_size("ctx"), lax.axis_size("batch")
    places = [(c, b) for c in range(size) for b in range(count)]
    return [
        lax.ppermute(
            array,
            ("ctx", "batch"),
            [(c * count + b, (c ^ m) * count + (b ^ 1)) for c, b in places],
        )
        for m, array in zip(offsets(), arrays)
    ]


def local(
    queries,
    latent_cache,
    token_latent,
    lengths,
    value_up_weight,
    out_proj,
    residual,
    norm_gain,
    router,
    expert_ids,
    expert_gate_up,
    expert_down,
    shared_gate_up,
    shared_down,
):
    ctx_index = lax.axis_index("ctx")
    ctx_count = lax.axis_size("ctx")
    batch_count = lax.axis_size("batch")
    batch_index = lax.axis_index("batch")
    _, rows, heads, width = queries.shape
    model = residual.shape[-1]
    experts = router.shape[1]
    total_rows = batch_count * rows
    shape = jax.ShapeDtypeStruct

    own_query = queries.reshape(rows * heads, width)
    every_query = [own_query] + swaps(own_query)
    other_token = crossings([token_latent[0]])[0]
    ids = expert_ids.transpose(1, 2, 0)
    picked, own_lengths = call(
        picked_kernel,
        (shape((total_rows, experts), F32), shape(lengths.shape, jnp.int32)),
        [
            pltpu.with_memory_space_constraint(ids, pltpu.HBM),
            pltpu.with_memory_space_constraint(lengths, pltpu.HBM),
        ],
        [HBM, HBM],
        scratch=[pltpu.VMEM(ids.shape, jnp.int32), pltpu.SemaphoreType.DMA((2,))],
        beside=[expert_gate_up],
    )
    valid = own_lengths - (ctx_index * latent_cache.shape[2]).astype(jnp.int32)
    places = jnp.stack([ctx_index * batch_count + batch_index, (batch_index ^ 1) * rows])
    marks = jnp.concatenate([valid, places.astype(jnp.int32)[None]], axis=1)
    *parts, picked = call(
        attend_kernel,
        [shape((rows * heads, width + 128), BF16)] * ctx_count
        + [shape((total_rows, experts), F32)],
        [marks, *every_query, latent_cache[0], token_latent[0], picked],
        beside=[expert_gate_up] * 3,
    )
    parts = crossings(parts)
    terms = call(
        project_kernel,
        shape((rows, model), BF16),
        [value_up_weight, out_proj, other_token, *parts[::-1]],
    )
    terms = crossings([terms] * ctx_count)
    hidden, copies = call(
        norm_kernel,
        (
            shape((rows, model), F32),
            shape((batch_count, rows, model), BF16),
        ),
        [residual[0], norm_gain, *terms],
        beside=[expert_gate_up] * 4,
    )

    every_rows = lax.all_to_all(copies, "batch", 0, 0)
    weighted, shared_part = call(
        expert_kernel,
        (
            shape((batch_count // 2, 2, rows, model), BF16),
            shape((rows, model), F32),
        ),
        [
            marks,
            every_rows,
            picked,
            router,
            expert_gate_up[0],
            expert_down[0],
            shared_gate_up,
            shared_down,
        ],
        scratch=[pltpu.VMEM((total_rows, expert_down.shape[1]), BF16)],
    )
    weighted = weighted.reshape(batch_count, rows, model)
    weighted = lax.all_to_all(weighted, "batch", 0, 0)
    totals = call(
        gather_sum_kernel, shape((rows, model), BF16), [weighted, shared_part]
    )
    totals = crossings([totals] * ctx_count)
    return call(final_kernel, shape((rows, model), BF16), [hidden, *totals])[None]


def solution(mesh):
    return jax.shard_map(
        local,
        mesh=mesh,
        in_specs=(
            P("batch", None, "ctx", None),
            P("batch", None, "ctx", None),
            P("batch", None, None),
            P("batch", None),
            P("ctx", None, None),
            P("ctx", None),
            P("batch", None, None),
            P(),
            P(),
            P(),
            P(("ctx", "batch"), None, None),
            P(("ctx", "batch"), None, None),
            P(None, None, "ctx"),
            P("ctx", None),
        ),
        out_specs=P("batch", None, None),
        check_vma=False,
    )
```

```python
import functools

import jax
import jax.numpy as jnp
from jax import lax
from jax.experimental import pallas as pl
from jax.experimental.pallas import tpu as pltpu
from jax.sharding import PartitionSpec as P

QK = 192
NEG_FILL = -1e30
ROUTE_SCALE = 2.446
EPSILON = 1e-06
SCALE = QK ** (-0.5)
LIMIT = 8 << 20
BF16, F32 = jnp.bfloat16, jnp.float32
VMEM = pl.BlockSpec(memory_space=pltpu.VMEM)
HBM = pl.BlockSpec(memory_space=pltpu.HBM)


def call(kernel, out_shape, args, specs=None, limit=LIMIT, scratch=(), beside=()):
    beside = [pltpu.with_memory_space_constraint(array, pltpu.HBM) for array in beside]
    count = len(args)

    def body(*refs):
        kernel(*refs[:count], *refs[count + len(beside) :])

    return pl.pallas_call(
        body,
        out_shape=out_shape,
        in_specs=(specs or [VMEM] * count) + [HBM] * len(beside),
        out_specs=jax.tree.map(lambda _: VMEM, out_shape),
        scratch_shapes=list(scratch),
        compiler_params=pltpu.CompilerParams(vmem_limit_bytes=limit),
    )(*args, *beside)


def split(value):
    high = value.astype(BF16).astype(F32)
    middle = (value - high).astype(BF16).astype(F32)
    return high, middle, value - high - middle


def tree_sum(refs):
    values = [ref[...].astype(F32) for ref in refs]
    while len(values) > 1:
        values = [a + b for a, b in zip(values[::2], values[1::2])]
    return values[0]


def by_heads(token, heads):
    token = token.astype(F32)
    rows, width = token.shape
    token = [jnp.broadcast_to(token[r : r + 1], (heads, width)) for r in range(rows)]
    return jnp.concatenate(token, axis=0)


def picked_kernel(ids_hbm, lengths_hbm, out_ref, lengths_ref, ids_ref, sems):
    copies = [
        pltpu.make_async_copy(ids_hbm, ids_ref, sems.at[0]),
        pltpu.make_async_copy(lengths_hbm, lengths_ref, sems.at[1]),
    ]
    for copy in copies:
        copy.start()
    for copy in copies:
        copy.wait()
    group, choices, count = ids_ref.shape
    total, experts = out_ref.shape
    expert = lax.broadcasted_iota(jnp.int32, (experts, count), 0)
    row = lax.broadcasted_iota(jnp.int32, (total, count), 0)
    batch = lax.broadcasted_iota(jnp.int32, (total, count), 1)
    picked = jnp.zeros((total, experts), F32)
    for r in range(group):
        named = jnp.zeros((experts, count), F32)
        for k in range(choices):
            named = jnp.where(ids_ref[r, k : k + 1, :] == expert, 1.0, named)
        place = (batch & 1) * (total // 2) + (batch >> 1) * group + r
        place = jnp.where(row == place, 1.0, 0.0).astype(BF16)
        picked = picked + lax.dot_general(
            place, named.astype(BF16), (((1,), (1,)), ((), ())), preferred_element_type=F32
        )
    out_ref[...] = picked


def attend_kernel(marks_ref, *refs):
    count = (len(refs) - 4) // 2
    q_refs, part_refs = refs[:count], refs[count + 3 : -1]
    cache_ref, token_ref, picked_ref = refs[count : count + 3]
    refs[-1][...] = picked_ref[...]
    rows, span, width = cache_ref.shape
    heads = q_refs[0].shape[0] // rows
    total = count * heads
    every = [q_ref[...].astype(F32) for q_ref in q_refs]
    scores = []
    for r in range(rows):
        q = jnp.concatenate([q[r * heads : (r + 1) * heads] for q in every], axis=0).astype(BF16)
        scores.append(
            lax.dot_general(
                q, cache_ref[r], (((1,), (1,)), ((), ())), preferred_element_type=F32
            )
        )
    position = lax.broadcasted_iota(jnp.int32, (total, span), 1)
    probs, tails = [], []
    lane = lax.broadcasted_iota(jnp.int32, (total, 128), 1)
    for r in range(rows):
        valid = position < marks_ref[:, r : r + 1]
        score = jnp.where(valid, scores[r] * SCALE, NEG_FILL)
        peak = jnp.max(score, axis=-1, keepdims=True)
        prob = jnp.where(valid, jnp.exp(score - peak), 0.0).astype(BF16)
        mass = jnp.sum(prob.astype(F32), axis=-1, keepdims=True)
        probs.append(prob)
        tail = jnp.zeros((total, 128), F32)
        for place, piece in enumerate(split(peak) + split(mass)):
            tail = jnp.where(lane == place, piece, tail)
        tails.append(tail)
    blends = [jnp.dot(probs[r], cache_ref[r], preferred_element_type=F32) for r in range(rows)]
    for m, part_ref in enumerate(part_refs):
        there = slice(m * heads, (m + 1) * heads)
        part = jnp.concatenate([blend[there] for blend in blends])
        tail = jnp.concatenate([tail[there] for tail in tails])
        if m == 0:
            token = by_heads(token_ref[...], heads)
            fresh = jnp.sum(every[0] * token, axis=-1, keepdims=True) * SCALE
            for place, piece in enumerate(split(fresh), 6):
                tail = jnp.where(lane[: rows * heads] == place, piece, tail)
        part_ref[:, :width] = part.astype(BF16)
        part_ref[:, width:] = tail.astype(BF16)


def project_kernel(up_ref, proj_ref, token_ref, *refs):
    part_refs, out_ref = refs[-2::-1], refs[-1]
    heads, width, _ = up_ref.shape
    rows = out_ref.shape[0]
    token = by_heads(token_ref[...], heads)
    tails = [part_ref[:, width:].astype(F32) for part_ref in part_refs]
    peaks = [tail[:, 0:1] + (tail[:, 1:2] + tail[:, 2:3]) for tail in tails]
    masses = [tail[:, 3:4] + (tail[:, 4:5] + tail[:, 5:6]) for tail in tails]
    fresh = tails[0][:, 6:7] + (tails[0][:, 7:8] + tails[0][:, 8:9])
    top = functools.reduce(jnp.maximum, peaks, fresh)
    mass = jnp.exp(fresh - top).astype(BF16).astype(F32)
    blend = mass * token
    for there, peak, part_ref in zip(masses, peaks, part_refs):
        factor = jnp.exp(peak - top)
        mass = mass + there * factor
        blend = blend + part_ref[:, :width].astype(F32) * factor
    latent = (blend / mass).astype(BF16)
    head = lax.rem(
        lax.broadcasted_iota(jnp.int32, (rows * heads, up_ref.shape[2]), 0), jnp.int32(heads)
    )
    values = [
        jnp.where(head == h, jnp.dot(latent, up_ref[h], preferred_element_type=F32), 0.0).astype(
            BF16
        )
        for h in range(heads)
    ]
    values = jnp.concatenate(values, axis=1)
    step = 256
    for n in range(0, proj_ref.shape[1], step):
        terms = jnp.dot(values, proj_ref[:, n : n + step], preferred_element_type=F32)
        sums = [
            jnp.sum(terms[r * heads : (r + 1) * heads], axis=0, keepdims=True) for r in range(rows)
        ]
        sums = jnp.concatenate(sums, axis=0)
        out_ref[:, n : n + step] = sums.astype(BF16)


def norm_kernel(residual_ref, gain_ref, *refs):
    hidden_ref, copies_ref = refs[-2:]
    hidden = residual_ref[...].astype(F32) + tree_sum(refs[:-2])
    inverse = lax.rsqrt(jnp.mean(hidden * hidden, axis=-1, keepdims=True) + EPSILON)
    normed = (hidden * inverse * gain_ref[...].astype(F32)[None]).astype(BF16)
    hidden_ref[...] = hidden
    for b in range(copies_ref.shape[0]):
        copies_ref[b] = normed


def expert_kernel(
    marks_ref,
    own_rows_ref,
    other_rows_ref,
    picked_ref,
    router_ref,
    gate_up_ref,
    down_ref,
    shared_gate_up_ref,
    shared_down_ref,
    out_ref,
    shared_ref,
    act,
):
    count = act.shape[0]
    pairs, _, group, _ = out_ref.shape
    half = count // 2
    rows = jnp.concatenate(
        [
            rows_ref[...].astype(F32).reshape(half, rows_ref.shape[2])
            for rows_ref in (own_rows_ref, other_rows_ref)
        ]
    )
    rows = rows.astype(BF16)
    first = marks_ref[:, group + 1 : group + 2] == 0
    picked = picked_ref[...]
    picked = jnp.where(first, picked, jnp.concatenate([picked[half:], picked[:half]]))
    width, model = down_ref.shape
    logits = jnp.dot(rows, router_ref[...], preferred_element_type=F32)
    score = jnp.where(picked > 0, jax.nn.sigmoid(logits), 0.0)
    expert = lax.broadcasted_iota(jnp.int32, score.shape, 1)
    own = jnp.where(expert == marks_ref[:, group : group + 1], score, 0.0)
    own = jnp.sum(own, axis=-1, keepdims=True)
    weight = (ROUTE_SCALE * own / jnp.sum(score, axis=-1, keepdims=True)).astype(BF16).astype(F32)
    step = 256
    for n in range(0, width, step):
        gate = jnp.dot(rows, gate_up_ref[:, n : n + step], preferred_element_type=F32)
        up = jnp.dot(rows, gate_up_ref[:, width + n : width + n + step], preferred_element_type=F32)
        act[:, n : n + step] = (jax.nn.silu(gate) * up).astype(BF16)
    for n in range(0, model, step):
        answer = jnp.dot(act[...], down_ref[:, n : n + step], preferred_element_type=F32)
        answer = weight * answer.astype(BF16).astype(F32)
        mine, other = answer[:half], answer[half:]
        for core, part in enumerate(
            (jnp.where(first, other, mine), jnp.where(first, mine, other))
        ):
            out_ref[:, core, :, n : n + step] = part.reshape(pairs, group, step).astype(BF16)
    row = lax.broadcasted_iota(jnp.int32, (8, count), 0)
    column = lax.broadcasted_iota(jnp.int32, (8, count), 1)
    first_row = half + marks_ref[:, group + 2 : group + 3]
    chosen = jnp.where((row < group) & (column == first_row + row), 1.0, 0.0).astype(BF16)
    chosen = jnp.dot(chosen, rows, preferred_element_type=F32).astype(BF16)
    gate = jnp.dot(chosen, shared_gate_up_ref[0], preferred_element_type=F32)
    up = jnp.dot(chosen, shared_gate_up_ref[1], preferred_element_type=F32)
    shared = (jax.nn.silu(gate) * up).astype(BF16)
    shared = jnp.dot(shared, shared_down_ref[...], preferred_element_type=F32)
    shared_ref[...] = shared[:group]


def gather_sum_kernel(parts_ref, shared_ref, out_ref):
    total = jnp.sum(parts_ref[...].astype(F32), axis=0) + shared_ref[...]
    out_ref[...] = total.astype(BF16)


def final_kernel(hidden_ref, *refs):
    refs[-1][...] = (hidden_ref[...] + tree_sum(refs[:-1])).astype(BF16)


def offsets():
    return [m ^ (m >> 1) for m in range(lax.axis_size("ctx"))]


def swaps(array):
    size = lax.axis_size("ctx")
    return [
        lax.ppermute(array, "ctx", [(place, place ^ m) for place in range(size)])
        for m in offsets()[1:]
    ]


def crossings(arrays):
    size, count = lax.axis_size("ctx"), lax.axis_size("batch")
    places = [(c, b) for c in range(size) for b in range(count)]
    return [
        lax.ppermute(
            array,
            ("ctx", "batch"),
            [(c * count + b, (c ^ m) * count + (b ^ 1)) for c, b in places],
        )
        for m, array in zip(offsets(), arrays)
    ]


def local(
    queries,
    latent_cache,
    token_latent,
    lengths,
    value_up_weight,
    out_proj,
    residual,
    norm_gain,
    router,
    expert_ids,
    expert_gate_up,
    expert_down,
    shared_gate_up,
    shared_down,
):
    ctx_index = lax.axis_index("ctx")
    ctx_count = lax.axis_size("ctx")
    batch_count = lax.axis_size("batch")
    batch_index = lax.axis_index("batch")
    _, rows, heads, width = queries.shape
    model = residual.shape[-1]
    experts = router.shape[1]
    total_rows = batch_count * rows
    shape = jax.ShapeDtypeStruct

    own_query = queries.reshape(rows * heads, width)
    every_query = [own_query] + swaps(own_query)
    other_token = crossings([token_latent[0]])[0]
    ids = expert_ids.transpose(1, 2, 0)
    picked, own_lengths = call(
        picked_kernel,
        (shape((total_rows, experts), F32), shape(lengths.shape, jnp.int32)),
        [
            pltpu.with_memory_space_constraint(ids, pltpu.HBM),
            pltpu.with_memory_space_constraint(lengths, pltpu.HBM),
        ],
        [HBM, HBM],
        scratch=[pltpu.VMEM(ids.shape, jnp.int32), pltpu.SemaphoreType.DMA((2,))],
        beside=[expert_gate_up],
    )
    valid = own_lengths - (ctx_index * latent_cache.shape[2]).astype(jnp.int32)
    places = [ctx_index * batch_count + batch_index, batch_index & 1, (batch_index >> 1) * rows]
    places = jnp.stack(places)
    marks = jnp.concatenate([valid, places.astype(jnp.int32)[None]], axis=1)
    *parts, picked = call(
        attend_kernel,
        [shape((rows * heads, width + 128), BF16)] * ctx_count
        + [shape((total_rows, experts), F32)],
        [marks, *every_query, latent_cache[0], token_latent[0], picked],
        beside=[expert_gate_up] * 3,
    )
    parts = crossings(parts)
    terms = call(
        project_kernel,
        shape((rows, model), BF16),
        [value_up_weight, out_proj, other_token, *parts[::-1]],
    )
    terms = crossings([terms] * ctx_count)
    hidden, copies = call(
        norm_kernel,
        (
            shape((rows, model), F32),
            shape((batch_count // 2, rows, model), BF16),
        ),
        [residual[0], norm_gain, *terms],
        beside=[expert_gate_up] * 4,
    )

    groups = [
        [c * batch_count + b for b in range(core, batch_count, 2)]
        for c in range(ctx_count)
        for core in range(2)
    ]
    own_rows = lax.all_to_all(copies, ("ctx", "batch"), 0, 0, axis_index_groups=groups)
    other_rows = crossings([own_rows])[0]
    weighted, shared_part = call(
        expert_kernel,
        (
            shape((batch_count // 2, 2, rows, model), BF16),
            shape((rows, model), F32),
        ),
        [
            marks,
            own_rows,
            other_rows,
            picked,
            router,
            expert_gate_up[0],
            expert_down[0],
            shared_gate_up,
            shared_down,
        ],
        scratch=[pltpu.VMEM((total_rows, expert_down.shape[1]), BF16)],
    )
    weighted = weighted.reshape(batch_count, rows, model)
    weighted = lax.all_to_all(weighted, "batch", 0, 0)
    totals = call(
        gather_sum_kernel, shape((rows, model), BF16), [weighted, shared_part]
    )
    totals = crossings([totals] * ctx_count)
    return call(final_kernel, shape((rows, model), BF16), [hidden, *totals])[None]


def solution(mesh):
    return jax.shard_map(
        local,
        mesh=mesh,
        in_specs=(
            P("batch", None, "ctx", None),
            P("batch", None, "ctx", None),
            P("batch", None, None),
            P("batch", None),
            P("ctx", None, None),
            P("ctx", None),
            P("batch", None, None),
            P(),
            P(),
            P(),
            P(("ctx", "batch"), None, None),
            P(("ctx", "batch"), None, None),
            P(None, None, "ctx"),
            P("ctx", None),
        ),
        out_specs=P("batch", None, None),
        check_vma=False,
    )
```

```python
import functools

import jax
import jax.numpy as jnp
from jax import lax
from jax.experimental import pallas as pl
from jax.experimental.pallas import tpu as pltpu
from jax.sharding import PartitionSpec as P

QK = 192
NEG_FILL = -1e30
ROUTE_SCALE = 2.446
EPSILON = 1e-06
SCALE = QK ** (-0.5)
LIMIT = 8 << 20
BF16, F32 = jnp.bfloat16, jnp.float32
VMEM = pl.BlockSpec(memory_space=pltpu.VMEM)
HBM = pl.BlockSpec(memory_space=pltpu.HBM)


def call(kernel, out_shape, args, specs=None, limit=LIMIT, scratch=(), beside=()):
    beside = [pltpu.with_memory_space_constraint(array, pltpu.HBM) for array in beside]
    count = len(args)

    def body(*refs):
        kernel(*refs[:count], *refs[count + len(beside) :])

    return pl.pallas_call(
        body,
        out_shape=out_shape,
        in_specs=(specs or [VMEM] * count) + [HBM] * len(beside),
        out_specs=jax.tree.map(lambda _: VMEM, out_shape),
        scratch_shapes=list(scratch),
        compiler_params=pltpu.CompilerParams(vmem_limit_bytes=limit),
    )(*args, *beside)


def split(value):
    high = value.astype(BF16).astype(F32)
    middle = (value - high).astype(BF16).astype(F32)
    return high, middle, value - high - middle


def tree_sum(refs):
    values = [ref[...].astype(F32) for ref in refs]
    while len(values) > 1:
        values = [a + b for a, b in zip(values[::2], values[1::2])]
    return values[0]


def by_heads(token, heads):
    token = token.astype(F32)
    rows, width = token.shape
    token = [jnp.broadcast_to(token[r : r + 1], (heads, width)) for r in range(rows)]
    return jnp.concatenate(token, axis=0)


def picked_kernel(ids_hbm, lengths_hbm, out_ref, lengths_ref, ids_ref, sems):
    copies = [
        pltpu.make_async_copy(ids_hbm, ids_ref, sems.at[0]),
        pltpu.make_async_copy(lengths_hbm, lengths_ref, sems.at[1]),
    ]
    for copy in copies:
        copy.start()
    for copy in copies:
        copy.wait()
    group, choices, count = ids_ref.shape
    total, experts = out_ref.shape
    expert = lax.broadcasted_iota(jnp.int32, (experts, count), 0)
    row = lax.broadcasted_iota(jnp.int32, (total, count), 0)
    batch = lax.broadcasted_iota(jnp.int32, (total, count), 1)
    picked = jnp.zeros((total, experts), F32)
    for r in range(group):
        named = jnp.zeros((experts, count), F32)
        for k in range(choices):
            named = jnp.where(ids_ref[r, k : k + 1, :] == expert, 1.0, named)
        place = (batch & 1) * (total // 2) + (batch >> 1) * group + r
        place = jnp.where(row == place, 1.0, 0.0).astype(BF16)
        picked = picked + lax.dot_general(
            place, named.astype(BF16), (((1,), (1,)), ((), ())), preferred_element_type=F32
        )
    out_ref[...] = picked


def attend_kernel(marks_ref, *refs):
    count = (len(refs) - 4) // 2
    q_refs, part_refs = (refs[0], *refs[count - 1 : 0 : -1]), refs[count + 3 : -1]
    cache_ref, token_ref, picked_ref = refs[count : count + 3]
    refs[-1][...] = picked_ref[...]
    rows, span, width = cache_ref.shape
    heads = q_refs[0].shape[0] // rows
    total = count * heads
    every = [q_ref[...].astype(F32) for q_ref in q_refs]
    scores = []
    for r in range(rows):
        q = jnp.concatenate([q[r * heads : (r + 1) * heads] for q in every], axis=0).astype(BF16)
        scores.append(
            lax.dot_general(
                q, cache_ref[r], (((1,), (1,)), ((), ())), preferred_element_type=F32
            )
        )
    position = lax.broadcasted_iota(jnp.int32, (total, span), 1)
    probs, tails = [], []
    lane = lax.broadcasted_iota(jnp.int32, (total, 128), 1)
    for r in range(rows):
        valid = position < marks_ref[:, r : r + 1]
        score = jnp.where(valid, scores[r] * SCALE, NEG_FILL)
        peak = jnp.max(score, axis=-1, keepdims=True)
        prob = jnp.where(valid, jnp.exp(score - peak), 0.0).astype(BF16)
        mass = jnp.sum(prob.astype(F32), axis=-1, keepdims=True)
        probs.append(prob)
        tail = jnp.zeros((total, 128), F32)
        for place, piece in enumerate(split(peak) + split(mass)):
            tail = jnp.where(lane == place, piece, tail)
        tails.append(tail)
    blends = [jnp.dot(probs[r], cache_ref[r], preferred_element_type=F32) for r in range(rows)]
    for m, part_ref in enumerate(part_refs):
        there = slice(m * heads, (m + 1) * heads)
        part = jnp.concatenate([blend[there] for blend in blends])
        tail = jnp.concatenate([tail[there] for tail in tails])
        if m == 0:
            token = by_heads(token_ref[...], heads)
            fresh = jnp.sum(every[0] * token, axis=-1, keepdims=True) * SCALE
            for place, piece in enumerate(split(fresh), 6):
                tail = jnp.where(lane[: rows * heads] == place, piece, tail)
        part_ref[:, :width] = part.astype(BF16)
        part_ref[:, width:] = tail.astype(BF16)


def project_kernel(up_ref, proj_ref, token_ref, *refs):
    part_refs, out_ref = refs[-2::-1], refs[-1]
    heads, width, _ = up_ref.shape
    rows = out_ref.shape[0]
    token = by_heads(token_ref[...], heads)
    tails = [part_ref[:, width:].astype(F32) for part_ref in part_refs]
    peaks = [tail[:, 0:1] + (tail[:, 1:2] + tail[:, 2:3]) for tail in tails]
    masses = [tail[:, 3:4] + (tail[:, 4:5] + tail[:, 5:6]) for tail in tails]
    fresh = tails[0][:, 6:7] + (tails[0][:, 7:8] + tails[0][:, 8:9])
    top = functools.reduce(jnp.maximum, peaks, fresh)
    mass = jnp.exp(fresh - top).astype(BF16).astype(F32)
    blend = mass * token
    for there, peak, part_ref in zip(masses, peaks, part_refs):
        factor = jnp.exp(peak - top)
        mass = mass + there * factor
        blend = blend + part_ref[:, :width].astype(F32) * factor
    latent = (blend / mass).astype(BF16)
    head = lax.rem(
        lax.broadcasted_iota(jnp.int32, (rows * heads, up_ref.shape[2]), 0), jnp.int32(heads)
    )
    values = [
        jnp.where(head == h, jnp.dot(latent, up_ref[h], preferred_element_type=F32), 0.0).astype(
            BF16
        )
        for h in range(heads)
    ]
    values = jnp.concatenate(values, axis=1)
    step = 256
    for n in range(0, proj_ref.shape[1], step):
        terms = jnp.dot(values, proj_ref[:, n : n + step], preferred_element_type=F32)
        sums = [
            jnp.sum(terms[r * heads : (r + 1) * heads], axis=0, keepdims=True) for r in range(rows)
        ]
        sums = jnp.concatenate(sums, axis=0)
        out_ref[:, n : n + step] = sums.astype(BF16)


def norm_kernel(residual_ref, gain_ref, *refs):
    hidden_ref, copies_ref = refs[-2:]
    hidden = residual_ref[...].astype(F32) + tree_sum(refs[:-2])
    inverse = lax.rsqrt(jnp.mean(hidden * hidden, axis=-1, keepdims=True) + EPSILON)
    normed = (hidden * inverse * gain_ref[...].astype(F32)[None]).astype(BF16)
    hidden_ref[...] = hidden
    for b in range(copies_ref.shape[0]):
        copies_ref[b] = normed


def expert_kernel(
    marks_ref,
    own_rows_ref,
    other_rows_ref,
    picked_ref,
    router_ref,
    gate_up_ref,
    down_ref,
    keep_ref,
    send_ref,
    act,
):
    count = act.shape[0]
    pairs, group, _ = keep_ref.shape
    half = count // 2
    rows = jnp.concatenate(
        [
            rows_ref[...].astype(F32).reshape(half, rows_ref.shape[2])
            for rows_ref in (own_rows_ref, other_rows_ref)
        ]
    )
    rows = rows.astype(BF16)
    first = marks_ref[:, group + 1 : group + 2] == 0
    picked = picked_ref[...]
    picked = jnp.where(first, picked, jnp.concatenate([picked[half:], picked[:half]]))
    width, model = down_ref.shape
    logits = jnp.dot(rows, router_ref[...], preferred_element_type=F32)
    score = jnp.where(picked > 0, jax.nn.sigmoid(logits), 0.0)
    expert = lax.broadcasted_iota(jnp.int32, score.shape, 1)
    own = jnp.where(expert == marks_ref[:, group : group + 1], score, 0.0)
    own = jnp.sum(own, axis=-1, keepdims=True)
    weight = (ROUTE_SCALE * own / jnp.sum(score, axis=-1, keepdims=True)).astype(BF16).astype(F32)
    step = 256
    for n in range(0, width, step):
        gate = jnp.dot(rows, gate_up_ref[:, n : n + step], preferred_element_type=F32)
        up = jnp.dot(rows, gate_up_ref[:, width + n : width + n + step], preferred_element_type=F32)
        act[:, n : n + step] = (jax.nn.silu(gate) * up).astype(BF16)
    for n in range(0, model, step):
        answer = jnp.dot(act[...], down_ref[:, n : n + step], preferred_element_type=F32)
        answer = weight * answer.astype(BF16).astype(F32)
        for out_ref, part in ((send_ref, answer[:half]), (keep_ref, answer[half:])):
            out_ref[:, :, n : n + step] = part.reshape(pairs, group, step).astype(BF16)


def shared_kernel(marks_ref, rows_ref, gate_up_ref, down_ref, out_ref):
    pairs, group, model = rows_ref.shape
    count = pairs * group
    rows = rows_ref[...].astype(F32).reshape(count, model).astype(BF16)
    row = lax.broadcasted_iota(jnp.int32, (8, count), 0)
    column = lax.broadcasted_iota(jnp.int32, (8, count), 1)
    first_row = marks_ref[:, group + 2 : group + 3]
    chosen = jnp.where((row < group) & (column == first_row + row), 1.0, 0.0).astype(BF16)
    chosen = jnp.dot(chosen, rows, preferred_element_type=F32).astype(BF16)
    gate = jnp.dot(chosen, gate_up_ref[0], preferred_element_type=F32)
    up = jnp.dot(chosen, gate_up_ref[1], preferred_element_type=F32)
    act = (jax.nn.silu(gate) * up).astype(BF16)
    out_ref[...] = jnp.dot(act, down_ref[...], preferred_element_type=F32)[:group]


def add_kernel(one_ref, two_ref, shared_ref, out_ref, kept_ref):
    kept_ref[...] = shared_ref[...]
    out_ref[...] = (one_ref[...].astype(F32) + two_ref[...].astype(F32)).astype(BF16)


def gather_sum_kernel(parts_ref, shared_ref, out_ref):
    total = jnp.sum(parts_ref[...].astype(F32), axis=0) + shared_ref[...]
    out_ref[...] = total.astype(BF16)


def final_kernel(hidden_ref, *refs):
    refs[-1][...] = (hidden_ref[...] + tree_sum(refs[:-1])).astype(BF16)


def offsets():
    return [m ^ (m >> 1) for m in range(lax.axis_size("ctx"))]


def swaps(array):
    size = lax.axis_size("ctx")
    return [
        lax.ppermute(array, "ctx", [(place, place ^ m) for place in range(size)])
        for m in offsets()[1:]
    ]


def crossings(arrays):
    size, count = lax.axis_size("ctx"), lax.axis_size("batch")
    places = [(c, b) for c in range(size) for b in range(count)]
    return [
        lax.ppermute(
            array,
            ("ctx", "batch"),
            [(c * count + b, (c ^ m) * count + (b ^ 1)) for c, b in places],
        )
        for m, array in zip(offsets(), arrays)
    ]


def local(
    queries,
    latent_cache,
    token_latent,
    lengths,
    value_up_weight,
    out_proj,
    residual,
    norm_gain,
    router,
    expert_ids,
    expert_gate_up,
    expert_down,
    shared_gate_up,
    shared_down,
):
    ctx_index = lax.axis_index("ctx")
    ctx_count = lax.axis_size("ctx")
    batch_count = lax.axis_size("batch")
    batch_index = lax.axis_index("batch")
    _, rows, heads, width = queries.shape
    model = residual.shape[-1]
    experts = router.shape[1]
    total_rows = batch_count * rows
    shape = jax.ShapeDtypeStruct

    own_query = queries.reshape(rows * heads, width)
    every_query = [own_query] + swaps(own_query)
    other_token = crossings([token_latent[0]])[0]
    ids = expert_ids.transpose(1, 2, 0)
    picked, own_lengths = call(
        picked_kernel,
        (shape((total_rows, experts), F32), shape(lengths.shape, jnp.int32)),
        [
            pltpu.with_memory_space_constraint(ids, pltpu.HBM),
            pltpu.with_memory_space_constraint(lengths, pltpu.HBM),
        ],
        [HBM, HBM],
        scratch=[pltpu.VMEM(ids.shape, jnp.int32), pltpu.SemaphoreType.DMA((2,))],
        beside=[expert_gate_up],
    )
    valid = own_lengths - (ctx_index * latent_cache.shape[2]).astype(jnp.int32)
    places = [ctx_index * batch_count + batch_index, batch_index & 1, (batch_index >> 1) * rows]
    places = jnp.stack(places)
    marks = jnp.concatenate([valid, places.astype(jnp.int32)[None]], axis=1)
    *parts, picked = call(
        attend_kernel,
        [shape((rows * heads, width + 128), BF16)] * ctx_count
        + [shape((total_rows, experts), F32)],
        [marks, own_query, *every_query[:0:-1], latent_cache[0], token_latent[0], picked],
        beside=[expert_gate_up] * 3,
    )
    parts = crossings(parts)
    terms = call(
        project_kernel,
        shape((rows, model), BF16),
        [value_up_weight, out_proj, other_token, *parts[::-1]],
    )
    terms = crossings([terms] * ctx_count)
    hidden, copies = call(
        norm_kernel,
        (
            shape((rows, model), F32),
            shape((batch_count // 2, rows, model), BF16),
        ),
        [residual[0], norm_gain, *terms[::-1]],
        beside=[expert_gate_up] * 4,
    )

    groups = [
        [c * batch_count + b for b in range(core, batch_count, 2)]
        for c in range(ctx_count)
        for core in range(2)
    ]
    own_rows = lax.all_to_all(copies, ("ctx", "batch"), 0, 0, axis_index_groups=groups)
    other_rows = crossings([own_rows])[0]
    keep, send = call(
        expert_kernel,
        (
            shape((batch_count // 2, rows, model), BF16),
            shape((batch_count // 2, rows, model), BF16),
        ),
        [
            marks,
            own_rows,
            other_rows,
            picked,
            router,
            expert_gate_up[0],
            expert_down[0],
        ],
        scratch=[pltpu.VMEM((total_rows, expert_down.shape[1]), BF16)],
    )
    shared_part = call(
        shared_kernel,
        shape((rows, model), F32),
        [marks, other_rows, shared_gate_up, shared_down],
    )
    weighted, shared_part = call(
        add_kernel,
        (shape((batch_count // 2, rows, model), BF16), shape((rows, model), F32)),
        [keep, crossings([send])[0], shared_part],
    )
    weighted = lax.all_to_all(weighted, ("ctx", "batch"), 0, 0, axis_index_groups=groups)
    totals = call(
        gather_sum_kernel, shape((rows, model), BF16), [weighted, shared_part]
    )
    totals = crossings([totals] * ctx_count)
    return call(final_kernel, shape((rows, model), BF16), [hidden, *totals[::-1]])[None]


def solution(mesh):
    return jax.shard_map(
        local,
        mesh=mesh,
        in_specs=(
            P("batch", None, "ctx", None),
            P("batch", None, "ctx", None),
            P("batch", None, None),
            P("batch", None),
            P("ctx", None, None),
            P("ctx", None),
            P("batch", None, None),
            P(),
            P(),
            P(),
            P(("ctx", "batch"), None, None),
            P(("ctx", "batch"), None, None),
            P(None, None, "ctx"),
            P("ctx", None),
        ),
        out_specs=P("batch", None, None),
        check_vma=False,
    )
```
